32 devices in a mesh: dp: 4 (over z), row: 2 (over x), col: 4 (over y, core).
Axes of the slice: x: 2, y: 2, z: 4, core: 2. Of those that a mesh axis runs over, the one named last changes fastest.
Arguments:
- tokens: bfloat16 [16, 1024, 1024], P(('dp', 'row'), None, 'col'), may hold values from -6 to 6
- segments: int32 [16, 1024], P(('dp', 'row')), may hold values from 0 to 2, as said below
- w_qkv: bfloat16 [1024, 3072], P('row', 'col'), may hold values from -0.1875 to 0.1875
- qv_bias: float32 [2048], P('col'), may hold values from -1.2 to 1.2
- w_out: bfloat16 [1024, 1024], P('col', 'row'), may hold values from -0.75 to 0.75
- out_bias: float32 [1024], P('col'), may hold values from -3 to 3
- gain_one: float32 [1024], P('col'), may hold values from 0.1 to 1.9
- shift_one: float32 [1024], P('col'), may hold values from -3 to 3
- w_in: bfloat16 [1024, 4096], P('row', 'col'), may hold values from -0.1875 to 0.1875
- in_bias: float32 [4096], P('col'), may hold values from -3 to 3
- w_down: bfloat16 [4096, 1024], P('col', 'row'), may hold values from -0.09375 to 0.09375
- down_bias: float32 [1024], P('col'), may hold values from -3 to 3
- gain_two: float32 [1024], P('col'), may hold values from 0.1 to 1.9
- shift_two: float32 [1024], P('col'), may hold values from -3 to 3
- cotangent: bfloat16 [16, 1024, 1024], P(('dp', 'row'), None, 'col'), may hold values from -6 to 6
Outputs:
- output: bfloat16 [16, 1024, 1024], P(('dp', 'row'), None, 'col')
- grad_tokens: bfloat16 [16, 1024, 1024], P(('dp', 'row'), None, 'col')
- grad_w_qkv: float32 [1024, 3072], P('row', 'col')
- grad_qv_bias: float32 [2048], P('col')
- grad_w_out: float32 [1024, 1024], P('col', 'row')
- grad_out_bias: float32 [1024], P('col')
- grad_gain_one: float32 [1024], P('col')
- grad_shift_one: float32 [1024], P('col')
- grad_w_in: float32 [1024, 4096], P('row', 'col')
- grad_in_bias: float32 [4096], P('col')
- grad_w_down: float32 [4096, 1024], P('col', 'row')
- grad_down_bias: float32 [1024], P('col')
- grad_gain_two: float32 [1024], P('col')
- grad_shift_two: float32 [1024], P('col')
The draws below stay inside these ranges and needn't reach their ends.
Inputs may be any that keep to these rules, and one draw needn't show every extreme that they name: `segments`: each row is one packed sequence: 0 at its first position, never falling, rising by at most one from a position to the next; no document begins within 128 positions of position 512. Positions 1022 and 1023 each raise the number unless it is already 2; the number never exceeds 2, so all positions numbered 2 attend to one another as one block.
All inputs are finite; a program needn't handle non-finite values.
Results may differ from the reference program's by a relative error of at most 0.019.
Values may be sent and summed in bfloat16 or wider, within the bound.
No kernel may reach another device: no remote copies, remote signals or barrier semaphores. Data moves between devices by JAX's collectives and lax.ppermute only.
A program may use at most 192 MiB of HBM per device.

```python
import math
import jax
import jax.numpy as jnp
from jax import lax

D = 1024
FF = 4096
HEADS = 16
HEAD_DIM = 64
SEQ = 1024
NSEQ = 16


def draw_segments(key, part):
    key = jax.random.fold_in(key, 7)
    random_rolls = jax.random.randint(key, (NSEQ, SEQ), 0, max(4, SEQ // 5))
    positions = jnp.arange(SEQ)
    center = SEQ // 2
    radius = max(1, SEQ // 8)
    allowed_cut = (positions > 0) & (jnp.abs(positions - center) > radius)
    forced_cut = positions >= SEQ - 2
    boundary = jnp.where(allowed_cut[None, :] & (random_rolls == 0) | forced_cut[None, :], 1, 0).astype(jnp.int32)
    return jnp.minimum(jnp.cumsum(boundary, axis=1), 2).astype(jnp.int32)


def block_scale(own_key, dims, pieces, smallest, largest):
    factor_of, own = 1.0, jax.random.fold_in(own_key, 6)
    for position, blocks in pieces:
        steps = jnp.exp(jax.random.uniform(jax.random.fold_in(own, position), (blocks,), jnp.float32, smallest / len(pieces), largest / len(pieces)))
        factor_of = factor_of * jnp.repeat(steps, dims[position] // blocks).reshape([-1 if axis == position else 1 for axis in range(len(dims))])
    return factor_of


def bell_draw(rng, shape, scale, most, pieces=(), dtype=jnp.bfloat16):
    loudness = block_scale(rng, shape, pieces, -0.22, 0.18) if pieces else 1.0
    drawn = jax.random.normal(rng, shape, jnp.float32) * scale * loudness
    return jnp.minimum(jnp.maximum(drawn, -most), most).astype(dtype)


def setup_inputs(seed: int = 0) -> dict:
    arg_keys = jax.random.split(jax.random.key(seed), 16)
    return {
        "tokens": bell_draw(arg_keys[0], (NSEQ, SEQ, D), 1.0, 6.0, ((0, 8), (2, 4))),
        "segments": draw_segments(jax.random.fold_in(arg_keys[15], 71), 0),
        "w_qkv": bell_draw(arg_keys[2], (D, 3 * D), D ** -0.5, 0.1875, ((0, 2), (1, 4))),
        "qv_bias": bell_draw(arg_keys[3], (2 * D,), 0.2, 1.2, ((0, 4),), jnp.float32),
        "w_out": bell_draw(arg_keys[4], (D, D), (D // 16) ** -0.5, 0.75, ((0, 4), (1, 2))),
        "out_bias": bell_draw(arg_keys[5], (D,), 0.5, 3.0, ((0, 4),), jnp.float32),
        "gain_one": jnp.clip(1.0 + 0.18 * jax.random.normal(arg_keys[6], (D,), jnp.float32), 0.1, 1.9),
        "shift_one": bell_draw(arg_keys[7], (D,), 0.5, 3.0, ((0, 4),), jnp.float32),
        "w_in": bell_draw(arg_keys[8], (D, FF), D ** -0.5, 0.1875, ((0, 2), (1, 4))),
        "in_bias": bell_draw(arg_keys[9], (FF,), 0.5, 3.0, ((0, 4),), jnp.float32),
        "w_down": bell_draw(arg_keys[10], (FF, D), FF ** -0.5, 0.09375, ((0, 4), (1, 2))),
        "down_bias": bell_draw(arg_keys[11], (D,), 0.5, 3.0, ((0, 4),), jnp.float32),
        "gain_two": jnp.clip(1.0 + 0.18 * jax.random.normal(arg_keys[12], (D,), jnp.float32), 0.1, 1.9),
        "shift_two": bell_draw(arg_keys[13], (D,), 0.5, 3.0, ((0, 4),), jnp.float32),
        "cotangent": bell_draw(arg_keys[14], (NSEQ, SEQ, D), 1.0, 6.0, ((0, 8), (2, 4))),
    }


epsilon = 1e-12
highest = lax.Precision.HIGHEST

@jax.custom_vjp
def low(v):
    return lax.optimization_barrier(v.astype(jnp.bfloat16)).astype(jnp.float32)

@jax.custom_vjp
def low_back(v):
    return v

def low_keep(v):
    return (low(v), None)

def low_pass(kept, grad):
    return (grad,)

def back_keep(v):
    return (v, None)

def back_low(kept, grad):
    return (low(grad),)
low.defvjp(low_keep, low_pass)
low_back.defvjp(back_keep, back_low)

def product(left, right):
    return jnp.dot(left, right, precision=highest, preferred_element_type=jnp.float32)

def norm_rows(values, gain, shift):
    row_mean = lax.optimization_barrier(jnp.mean(values, axis=-1, keepdims=True))
    centered = values - row_mean
    row_var = lax.optimization_barrier(jnp.mean(centered * centered, axis=-1, keepdims=True))
    return centered * lax.rsqrt(row_var + epsilon) * gain + shift

def encoder_layer(layer_in, segment, weights):
    w_qkv, qv_bias, w_out, out_bias, gain_one, shift_one, w_in, in_bias, w_down, down_bias, gain_two, shift_two = weights
    qv_pairs = qv_bias.reshape(HEADS, 2, HEAD_DIM)
    bias_full = jnp.stack([qv_pairs[:, 0], jnp.zeros_like(qv_pairs[:, 0]), qv_pairs[:, 1]], axis=1).reshape(3 * D)
    projected = low(low_back(product(layer_in, w_qkv) + bias_full)).reshape(SEQ, HEADS, 3, HEAD_DIM)
    score_scale = 1.0 / math.sqrt(HEAD_DIM)
    scores = jnp.einsum('qhd,khd->hqk', projected[:, :, 0], projected[:, :, 1], precision=highest) * score_scale
    same_doc = segment[:, None] == segment[None, :]
    scores = low_back(jnp.where(same_doc[None], scores, -1000000000.0))
    probs_low = low(jax.nn.softmax(scores, axis=-1))
    mixed_heads = low(low_back(jnp.einsum('hqk,khd->qhd', probs_low, projected[:, :, 2], precision=highest))).reshape(SEQ, D)
    attention = low_back(product(mixed_heads, w_out) + out_bias)
    normed_one = norm_rows(layer_in + attention, gain_one, shift_one)
    hidden_pre = low_back(product(low(normed_one), w_in) + in_bias)
    hidden_act = low(jax.nn.gelu(hidden_pre, approximate=False))
    ffn_out = low_back(product(hidden_act, w_down) + down_bias)
    return norm_rows(normed_one + ffn_out, gain_two, shift_two)

def reference(tokens, segments, w_qkv, qv_bias, w_out, out_bias, gain_one, shift_one, w_in, in_bias, w_down, down_bias, gain_two, shift_two, cotangent):
    weights = tuple((weight.astype(jnp.float32) for weight in (w_qkv, qv_bias, w_out, out_bias, gain_one, shift_one, w_in, in_bias, w_down, down_bias, gain_two, shift_two)))

    def through(grad_total, sequence):
        seq_tokens, seq_segments, seq_cotangent = sequence

        def forward(layer_in, layer_weights):
            return encoder_layer(layer_in, seq_segments, layer_weights)
        seq_output, pullback = jax.vjp(forward, seq_tokens.astype(jnp.float32), weights)
        grad_seq, grad_weights = pullback(seq_cotangent.astype(jnp.float32))
        grad_total = jax.tree.map(jnp.add, grad_total, grad_weights)
        return (grad_total, (seq_output.astype(jnp.bfloat16), grad_seq.astype(jnp.bfloat16)))
    start_total = jax.tree.map(jnp.zeros_like, weights)
    grad_total, (output, grad_tokens) = lax.scan(through, start_total, (tokens, segments, cotangent))
    g_qkv, g_qv, g_out, g_obias, g_gone, g_sone, g_in, g_ibias, g_down, g_dbias, g_gtwo, g_stwo = grad_total
    return (output, grad_tokens, g_qkv, g_qv, g_out, g_obias, g_gone, g_sone, g_in, g_ibias, g_down, g_dbias, g_gtwo, g_stwo)
```

```python
import functools
import math

import jax
import jax.numpy as jnp
from jax import lax
from jax.experimental import pallas as pl
from jax.experimental.pallas import tpu as pltpu
from jax.sharding import PartitionSpec as P

HEAD_DIM = 64
epsilon = 1e-12
f32 = jnp.float32
bf16 = jnp.bfloat16
NT = (((1,), (1,)), ((), ()))
NN = (((1,), (0,)), ((), ()))
TN = (((0,), (0,)), ((), ()))


def mm(left, right, dims=NN):
    return lax.dot_general(left, right, dims, preferred_element_type=f32)


def to_core(values):
    size = lax.axis_size("col")
    return lax.ppermute(values, "col", [(i, i ^ 1) for i in range(size)])


def to_chip(values):
    size = lax.axis_size("col")
    return lax.ppermute(values, "col", [(i, i ^ 2) for i in range(size)])


def to_row(values):
    return lax.ppermute(values, "row", [(0, 1), (1, 0)])


def attend_kernel(chunk, qkv_ref, mask_ref, exp_ref, mixed_ref, inv_ref):
    count = qkv_ref.shape[0]
    ones = jnp.ones((count, HEAD_DIM), bf16)
    for head in range(2):
        base = 3 * HEAD_DIM * head
        cols = slice(head * HEAD_DIM, (head + 1) * HEAD_DIM)
        query = qkv_ref[:, base : base + HEAD_DIM] * bf16(1.0 / math.sqrt(HEAD_DIM))
        key = qkv_ref[:, base + HEAD_DIM : base + 2 * HEAD_DIM]
        value = qkv_ref[:, base + 2 * HEAD_DIM : base + 3 * HEAD_DIM]
        query = jnp.concatenate([query, mask_ref[:, :HEAD_DIM]], axis=1)
        key = jnp.concatenate([key, mask_ref[:, HEAD_DIM:]], axis=1)
        value = jnp.concatenate([value, ones], axis=1)
        for start in range(0, count, chunk):
            rows = slice(start, start + chunk)
            scores = mm(query[rows], key, NT)
            top = jnp.max(scores, axis=-1, keepdims=True)
            exponent = jnp.exp(scores - top).astype(bf16)
            exp_ref[head, rows, :] = exponent
            mixed = mm(exponent, value)
            inverse = 1.0 / mixed[:, HEAD_DIM:]
            mixed_ref[rows, cols] = (mixed[:, :HEAD_DIM] * inverse).astype(bf16)
            inv_ref[rows, cols] = inverse


def attend(qkv, mask):
    count, width = qkv.shape
    pairs = width // (6 * HEAD_DIM)
    return pl.pallas_call(
        functools.partial(attend_kernel, min(512, count)),
        grid=(pairs,),
        in_specs=[
            pl.BlockSpec((count, 6 * HEAD_DIM), lambda p: (0, p)),
            pl.BlockSpec((count, 2 * HEAD_DIM), lambda p: (0, 0)),
        ],
        out_specs=[
            pl.BlockSpec((2, count, count), lambda p: (p, 0, 0)),
            pl.BlockSpec((count, 2 * HEAD_DIM), lambda p: (0, p)),
            pl.BlockSpec((count, 2 * HEAD_DIM), lambda p: (0, p)),
        ],
        out_shape=[
            jax.ShapeDtypeStruct((2 * pairs, count, count), bf16),
            jax.ShapeDtypeStruct((count, 2 * HEAD_DIM * pairs), bf16),
            jax.ShapeDtypeStruct((count, 2 * HEAD_DIM * pairs), f32),
        ],
        compiler_params=pltpu.CompilerParams(vmem_limit_bytes=48 * 2**20),
        cost_estimate=pl.CostEstimate(
            flops=32 * pairs * count * count * HEAD_DIM,
            bytes_accessed=4 * pairs * count * count,
            transcendentals=2 * pairs * count * count,
        ),
        name="attend",
    )(qkv, mask)


def attend_back_kernel(chunk, qkv_ref, exp_ref, mixed_ref, inv_ref, grad_ref, out_ref):
    count = qkv_ref.shape[0]
    lane = lax.broadcasted_iota(jnp.int32, (count, HEAD_DIM), 1)
    minus = jnp.where(lane < 2, -1.0, 0.0).astype(bf16)
    scale = 1.0 / math.sqrt(HEAD_DIM)
    for head in range(2):
        base = 3 * HEAD_DIM * head
        cols = slice(head * HEAD_DIM, (head + 1) * HEAD_DIM)
        query = qkv_ref[:, base : base + HEAD_DIM]
        key = qkv_ref[:, base + HEAD_DIM : base + 2 * HEAD_DIM]
        value = qkv_ref[:, base + 2 * HEAD_DIM : base + 3 * HEAD_DIM]
        value = jnp.concatenate([value, minus], axis=1)
        scaled = grad_ref[:, cols].astype(f32) * inv_ref[:, cols]
        scaled_low = scaled.astype(bf16)
        inner = jnp.sum(scaled * mixed_ref[:, cols].astype(f32), axis=1, keepdims=True)
        inner_high = inner.astype(bf16).astype(f32)
        inner_pair = jnp.where(
            lane == 0, inner_high, jnp.where(lane == 1, inner - inner_high, 0.0)
        ).astype(bf16)
        wide = jnp.concatenate([scaled_low, inner_pair], axis=1)
        grad_key = grad_value = None
        for start in range(0, count, chunk):
            rows = slice(start, start + chunk)
            exponent = exp_ref[head, rows, :]
            grad_probs = mm(wide[rows], value, NT)
            grad_scores = (exponent.astype(f32) * grad_probs).astype(bf16)
            out_ref[rows, base : base + HEAD_DIM] = (mm(grad_scores, key) * scale).astype(bf16)
            key_part = mm(query[rows], grad_scores, TN)
            value_part = mm(scaled_low[rows], exponent, TN)
            grad_key = key_part if grad_key is None else grad_key + key_part
            grad_value = value_part if grad_value is None else grad_value + value_part
        out_ref[:, base + HEAD_DIM : base + 2 * HEAD_DIM] = (grad_key.T * scale).astype(bf16)
        out_ref[:, base + 2 * HEAD_DIM : base + 3 * HEAD_DIM] = grad_value.T.astype(bf16)


def attend_back(qkv, exponent, mixed, inverse, grad_mixed):
    count, width = qkv.shape
    pairs = width // (6 * HEAD_DIM)
    return pl.pallas_call(
        functools.partial(attend_back_kernel, min(512, count)),
        grid=(pairs,),
        in_specs=[
            pl.BlockSpec((count, 6 * HEAD_DIM), lambda p: (0, p)),
            pl.BlockSpec((2, count, count), lambda p: (p, 0, 0)),
        ]
        + [pl.BlockSpec((count, 2 * HEAD_DIM), lambda p: (0, p))] * 3,
        out_specs=pl.BlockSpec((count, 6 * HEAD_DIM), lambda p: (0, p)),
        out_shape=jax.ShapeDtypeStruct((count, width), bf16),
        compiler_params=pltpu.CompilerParams(vmem_limit_bytes=48 * 2**20),
        cost_estimate=pl.CostEstimate(
            flops=40 * pairs * count * count * HEAD_DIM,
            bytes_accessed=4 * pairs * count * count,
            transcendentals=0,
        ),
        name="attend_back",
    )(qkv, exponent, mixed, inverse, grad_mixed)


def normalize(values):
    centered = values - jnp.mean(values, axis=-1, keepdims=True)
    inverse = lax.rsqrt(jnp.mean(centered * centered, axis=-1, keepdims=True) + epsilon)
    return centered * inverse, inverse


def norm_back(grad_in, normed, inverse):
    return inverse * (
        grad_in
        - jnp.mean(grad_in, axis=-1, keepdims=True)
        - normed * jnp.mean(grad_in * normed, axis=-1, keepdims=True)
    )


def pick(values, index, axis):
    return lax.dynamic_index_in_dim(values, index, axis, keepdims=False)


def body(
    tokens, segments, w_qkv, qv_bias, w_out, out_bias, gain_one, shift_one,
    w_in, in_bias, w_down, down_bias, gain_two, shift_two, cotangent,
):
    row = lax.axis_index("row")
    col = lax.axis_index("col")
    chip, core = col // 2, col % 2
    same = row == chip
    first_core = core == 0
    seq_count, count, width = tokens.shape
    half = count // 2
    model = width * lax.axis_size("col")
    heads = qv_bias.shape[0] // (2 * HEAD_DIM)
    hidden = in_bias.shape[0]

    def by_half(mine, other):
        return jnp.where(same, mine, other), jnp.where(same, other, mine)

    mine = pick(tokens, chip, 0)
    pair = jnp.stack(by_half(mine, to_chip(pick(tokens, 1 - chip, 0))))
    pair = pair.reshape(2, 2, half, width)
    own, away = pick(pair, core, 1), pick(pair, 1 - core, 1)
    here = jnp.stack([own, away])
    there = to_core(jnp.stack([away, own]))
    even, odd = jnp.where(first_core, here, there), jnp.where(first_core, there, here)
    wide = jnp.stack([even, odd], axis=2)
    wide = wide.transpose(0, 3, 1, 2, 4).reshape(count, model)

    def small_gather(values):
        low, high = by_half(values, to_chip(values))
        both = jnp.stack([low, high], axis=1)
        other = to_core(both)
        even, odd = jnp.where(first_core, both, other), jnp.where(first_core, other, both)
        return jnp.stack([even, odd], axis=2).reshape(values.shape[0], model)

    vectors = small_gather(
        jnp.stack([out_bias, gain_one, shift_one, down_bias, gain_two, shift_two])
    )
    out_bias_w, gain_one_w, shift_one_w, down_bias_w, gain_two_w, shift_two_w = vectors
    qv_pairs = qv_bias.reshape(heads, 2, HEAD_DIM)
    qkv_bias = jnp.stack(
        [qv_pairs[:, 0], jnp.zeros_like(qv_pairs[:, 0]), qv_pairs[:, 1]], axis=1
    ).reshape(-1)
    bias_pack = jnp.concatenate([qkv_bias, in_bias])
    bias_pack = [bias_pack, to_chip(bias_pack)]
    qkv_biases = [b[: 3 * heads * HEAD_DIM] for b in bias_pack]
    in_biases = [b[3 * heads * HEAD_DIM :] for b in bias_pack]

    segment = pick(segments, chip, 0).reshape(2, half)
    segment = jnp.concatenate([pick(segment, core, 0), pick(segment, 1 - core, 0)])
    ids = jnp.arange(HEAD_DIM)
    differs = jnp.where((segment[:, None] != ids) & (ids < 3), -(2.0**30), 0.0)
    mask = jnp.concatenate([differs, segment[:, None] == ids], axis=1).astype(bf16)

    qkv_mine = jnp.concatenate([w_qkv, to_row(w_qkv)], axis=0)
    qkv_near = to_chip(w_qkv)
    qkv_other = jnp.concatenate([qkv_near, to_row(qkv_near)], axis=0)
    out_row = to_row(w_out)
    out_mine = jnp.concatenate([w_out, out_row], axis=1)
    out_other = jnp.concatenate([to_chip(w_out), to_chip(out_row)], axis=1)
    in_mine = jnp.concatenate([w_in, to_row(w_in)], axis=0)
    in_near = to_chip(w_in)
    in_other = jnp.concatenate([in_near, to_row(in_near)], axis=0)
    down_row = to_row(w_down)
    down_mine = jnp.concatenate([w_down, down_row], axis=1)
    down_other = jnp.concatenate([to_chip(w_down), to_chip(down_row)], axis=1)
    w_qkvs, w_outs = [qkv_mine, qkv_other], [out_mine, out_other]
    w_ins, w_downs = [in_mine, in_other], [down_mine, down_other]

    cot = pick(cotangent, chip, 0)
    cot = jnp.stack(by_half(cot, to_chip(pick(cotangent, 1 - chip, 0))))
    cot = cot.reshape(2, 2, half, width)
    cot_here, cot_there = pick(cot, core, 1), to_core(pick(cot, 1 - core, 1))
    even = jnp.where(first_core, cot_here, cot_there)
    odd = jnp.where(first_core, cot_there, cot_here)
    cot = jnp.stack([even, odd], axis=1).transpose(2, 0, 1, 3).reshape(half, model)

    def core_scatter(lefts, rights, dims):
        other = sum(mm(l[half:], r, dims) for l, r in zip(lefts, rights))
        arrived = to_core(other.astype(bf16))
        own = sum(mm(l[:half], r, dims) for l, r in zip(lefts, rights))
        return own + arrived.astype(f32)

    def core_gather(values):
        return jnp.concatenate([values, to_core(values)], axis=0)

    qkvs = [(mm(wide, w) + b).astype(bf16) for w, b in zip(w_qkvs, qkv_biases)]
    attended = [attend(qkv, mask) for qkv in qkvs]
    mixed = [a[1] for a in attended]
    attention = core_scatter(mixed, w_outs, NN) + out_bias_w
    normed_one, inverse_one = normalize(wide[:half].astype(f32) + attention)
    first_out = normed_one * gain_one_w + shift_one_w
    first_wide = core_gather(first_out.astype(bf16))
    acts, slopes = [], []
    for w, b in zip(w_ins, in_biases):
        pre = mm(first_wide, w) + b
        cdf = 0.5 * (1.0 + lax.erf(pre * (1.0 / math.sqrt(2.0))))
        pdf = jnp.exp(-0.5 * pre * pre) * (1.0 / math.sqrt(2.0 * math.pi))
        acts.append((pre * cdf).astype(bf16))
        slopes.append((cdf + pre * pdf).astype(bf16))
    ffn_out = core_scatter(acts, w_downs, NN) + down_bias_w
    normed_two, inverse_two = normalize(first_out + ffn_out)
    output = (normed_two * gain_two_w + shift_two_w).astype(bf16)

    cot = cot.astype(f32)
    grad_gain_two = jnp.sum(cot * normed_two, axis=0)
    grad_shift_two = jnp.sum(cot, axis=0)
    grad_pre_two = norm_back(cot * gain_two_w, normed_two, inverse_two)
    grad_ffn = grad_pre_two.astype(bf16)
    grad_down_bias = jnp.sum(grad_ffn, axis=0, dtype=f32)
    grad_ffn_wide = core_gather(grad_ffn)
    grad_downs = [mm(a, grad_ffn_wide, TN).astype(bf16) for a in acts]
    grad_hiddens = [
        (mm(grad_ffn_wide, w, NT) * s.astype(f32)).astype(bf16) for w, s in zip(w_downs, slopes)
    ]
    grad_in_biases = [jnp.sum(g, axis=0, dtype=f32) for g in grad_hiddens]
    grad_normed = grad_pre_two + core_scatter(grad_hiddens, w_ins, NT)
    grad_ins = [mm(first_wide, g, TN).astype(bf16) for g in grad_hiddens]
    grad_gain_one = jnp.sum(grad_normed * normed_one, axis=0)
    grad_shift_one = jnp.sum(grad_normed, axis=0)
    grad_pre_one = norm_back(grad_normed * gain_one_w, normed_one, inverse_one)
    grad_attention = grad_pre_one.astype(bf16)
    grad_out_bias = jnp.sum(grad_attention, axis=0, dtype=f32)
    grad_attn_wide = core_gather(grad_attention)
    grad_outs = [mm(m, grad_attn_wide, TN).astype(bf16) for m in mixed]
    grad_mixed = [mm(grad_attn_wide, w, NT).astype(bf16) for w in w_outs]
    grad_qkvs = [
        attend_back(qkv, e, m, i, g)
        for qkv, (e, m, i), g in reversed(list(zip(qkvs, attended, grad_mixed)))
    ][::-1]
    grad_w_qkvs = [mm(wide, g, TN).astype(bf16) for g in reversed(grad_qkvs)][::-1]
    grad_wide = sum(mm(g, w, NT) for g, w in zip(grad_qkvs, w_qkvs))
    grad_wide = jnp.concatenate([grad_wide[:half] + grad_pre_one, grad_wide[half:]], axis=0)

    def chip_return(values):
        mine = jnp.where(same, values[:, 0], values[:, 1])
        away = jnp.where(same, values[:, 1], values[:, 0])
        arrived = to_chip(away)
        first = chip == 0
        return jnp.stack([jnp.where(first, mine, arrived), jnp.where(first, arrived, mine)])

    def token_order(own, other):
        return jnp.concatenate(
            [jnp.where(first_core, own, other), jnp.where(first_core, other, own)], axis=0
        )

    split = output.reshape(half, 2, 2, width)
    output = chip_return(token_order(pick(split, core, 2), to_core(pick(split, 1 - core, 2))))
    split = grad_wide.reshape(count, 2, 2, width)
    arrived = to_core(pick(split, 1 - core, 2).astype(bf16))
    arrived = jnp.concatenate([arrived[half:], arrived[:half]], axis=0)
    split = (pick(split, core, 2) + arrived.astype(f32)).astype(bf16)
    grad_tokens = chip_return(token_order(split[:half], split[half:]))

    def halves(values, axis):
        size = values.shape[axis] // 2
        return lax.slice_in_dim(values, 0, size, axis=axis), lax.slice_in_dim(
            values, size, 2 * size, axis=axis
        )

    def added(own, arrived):
        return (own.astype(f32) + arrived.astype(f32)).astype(bf16)

    def chip_first(mine, other, axis):
        own, away = halves(added(mine, to_chip(other)), axis)
        return added(own, to_row(away))

    def row_first(mine, other, axis):
        parts = [halves(v, axis) for v in (mine, other)]
        mine, other = [added(own, to_row(away)) for own, away in parts]
        return added(mine, to_chip(other))

    def over_dp(values):
        return lax.psum(values, "dp").astype(f32)

    grad_w_down = over_dp(row_first(*grad_downs, 1))
    grad_w_in = over_dp(chip_first(*grad_ins, 0))
    grad_w_out = over_dp(chip_first(*grad_outs, 1))
    cut = 3 * heads * HEAD_DIM // 2
    grad_w_qkv = over_dp(
        jnp.concatenate(
            [
                row_first(*[g[:, :cut] for g in grad_w_qkvs], 0),
                chip_first(*[g[:, cut:] for g in grad_w_qkvs], 0),
            ],
            axis=1,
        )
    )

    features = jnp.stack(
        [grad_out_bias, grad_gain_one, grad_shift_one, grad_down_bias, grad_gain_two, grad_shift_two]
    ).reshape(6, 2, 2, width)
    features = pick(features, core, 2) + to_core(pick(features, 1 - core, 2))
    feature_own = jnp.where(same, features[:, 0], features[:, 1])
    feature_away = jnp.where(same, features[:, 1], features[:, 0])
    qv_sums = []
    for g in grad_qkvs:
        sums = jnp.sum(g, axis=0, dtype=f32).reshape(heads, 3, HEAD_DIM)
        qv_sums.append(jnp.stack([sums[:, 0], sums[:, 2]], axis=1).reshape(-1))
    small = [
        jnp.concatenate([q, i, f.reshape(-1)])
        for q, i, f in zip(qv_sums, grad_in_biases, (feature_own, feature_away))
    ]
    small = lax.psum(small[0] + to_chip(small[1]), ("dp", "row"))
    qv_len = qv_bias.shape[0]
    g_qv, g_in = small[:qv_len], small[qv_len : qv_len + hidden]
    g_out, g_gone, g_sone, g_down, g_gtwo, g_stwo = small[qv_len + hidden :].reshape(6, width)
    return (
        output, grad_tokens, grad_w_qkv, g_qv, grad_w_out, g_out, g_gone, g_sone,
        grad_w_in, g_in, grad_w_down, g_down, g_gtwo, g_stwo,
    )


def solution(mesh):
    tokens = P(("dp", "row"), None, "col")
    feature = P("col")
    by_row, by_col = P("row", "col"), P("col", "row")
    return jax.shard_map(
        body,
        mesh=mesh,
        in_specs=(
            tokens, P(("dp", "row"), None), by_row, feature, by_col, feature, feature, feature,
            by_row, feature, by_col, feature, feature, feature, tokens,
        ),
        out_specs=(
            tokens, tokens, by_row, feature, by_col, feature, feature, feature,
            by_row, feature, by_col, feature, feature, feature,
        ),
        check_vma=False,
    )
```

```python
import functools
import math

import jax
import jax.numpy as jnp
from jax import lax
from jax.experimental import pallas as pl
from jax.experimental.pallas import tpu as pltpu
from jax.sharding import PartitionSpec as P

HEAD_DIM = 64
epsilon = 1e-12
f32 = jnp.float32
bf16 = jnp.bfloat16
NT = (((1,), (1,)), ((), ()))
NN = (((1,), (0,)), ((), ()))
TN = (((0,), (0,)), ((), ()))


QUICK = pl.CostEstimate(flops=1024, bytes_accessed=1024, transcendentals=0)


def mm(left, right, dims=NN):
    return lax.dot_general(left, right, dims, preferred_element_type=f32)


def to_core(values):
    size = lax.axis_size("col")
    return lax.ppermute(values, "col", [(i, i ^ 1) for i in range(size)])


def to_chip(values):
    size = lax.axis_size("col")
    return lax.ppermute(values, "col", [(i, i ^ 2) for i in range(size)])


def to_row(values):
    return lax.ppermute(values, "row", [(0, 1), (1, 0)])


def attend_kernel(chunk, wide_ref, left_ref, right_ref, bias_ref, mask_ref, qkv_ref, exp_ref, mixed_ref, inv_ref):
    count, side = wide_ref.shape[0], left_ref.shape[0]
    projected = mm(wide_ref[:, :side], left_ref[...]) + mm(wide_ref[:, side:], right_ref[...])
    qkv_ref[...] = (projected + bias_ref[...]).astype(bf16)
    ones = jnp.ones((count, HEAD_DIM), bf16)
    for head in range(2):
        base = 3 * HEAD_DIM * head
        cols = slice(head * HEAD_DIM, (head + 1) * HEAD_DIM)
        query = qkv_ref[:, base : base + HEAD_DIM] * bf16(1.0 / math.sqrt(HEAD_DIM))
        key = qkv_ref[:, base + HEAD_DIM : base + 2 * HEAD_DIM]
        value = qkv_ref[:, base + 2 * HEAD_DIM : base + 3 * HEAD_DIM]
        query = jnp.concatenate([query, mask_ref[:, :HEAD_DIM]], axis=1)
        key = jnp.concatenate([key, mask_ref[:, HEAD_DIM:]], axis=1)
        value = jnp.concatenate([value, ones], axis=1)
        for start in range(0, count, chunk):
            rows = slice(start, start + chunk)
            scores = mm(query[rows], key, NT)
            top = jnp.max(scores, axis=-1, keepdims=True)
            exponent = jnp.exp(scores - top).astype(bf16)
            exp_ref[head, rows, :] = exponent
            mixed = mm(exponent, value)
            inverse = 1.0 / mixed[:, HEAD_DIM:]
            mixed_ref[rows, cols] = (mixed[:, :HEAD_DIM] * inverse).astype(bf16)
            inv_ref[rows, cols] = inverse


def attend(wide, left, right, bias, mask):
    count, model = wide.shape
    side, width = left.shape
    six = 6 * HEAD_DIM
    pairs = width // six
    return pl.pallas_call(
        functools.partial(attend_kernel, min(512, count)),
        grid=(pairs,),
        in_specs=[
            pl.BlockSpec((count, model), lambda p: (0, 0)),
            pl.BlockSpec((side, six), lambda p: (0, p)),
            pl.BlockSpec((side, six), lambda p: (0, p)),
            pl.BlockSpec((1, six), lambda p: (0, p)),
            pl.BlockSpec((count, 2 * HEAD_DIM), lambda p: (0, 0)),
        ],
        out_specs=[
            pl.BlockSpec((count, six), lambda p: (0, p)),
            pl.BlockSpec((2, count, count), lambda p: (p, 0, 0)),
            pl.BlockSpec((count, 2 * HEAD_DIM), lambda p: (0, p)),
            pl.BlockSpec((count, 2 * HEAD_DIM), lambda p: (0, p)),
        ],
        out_shape=[
            jax.ShapeDtypeStruct((count, width), bf16),
            jax.ShapeDtypeStruct((2 * pairs, count, count), bf16),
            jax.ShapeDtypeStruct((count, 2 * HEAD_DIM * pairs), bf16),
            jax.ShapeDtypeStruct((count, 2 * HEAD_DIM * pairs), f32),
        ],
        compiler_params=pltpu.CompilerParams(vmem_limit_bytes=52 * 2**20),
        cost_estimate=QUICK,
        name="attend",
    )(wide, left, right, bias.reshape(1, width), mask)


def attend_back_kernel(chunk, qkv_ref, exp_ref, mixed_ref, inv_ref, grad_ref, out_ref):
    count = qkv_ref.shape[0]
    lane = lax.broadcasted_iota(jnp.int32, (count, HEAD_DIM), 1)
    minus = jnp.where(lane < 2, -1.0, 0.0).astype(bf16)
    scale = 1.0 / math.sqrt(HEAD_DIM)
    for head in range(2):
        base = 3 * HEAD_DIM * head
        cols = slice(head * HEAD_DIM, (head + 1) * HEAD_DIM)
        query = qkv_ref[:, base : base + HEAD_DIM]
        key = qkv_ref[:, base + HEAD_DIM : base + 2 * HEAD_DIM]
        value = qkv_ref[:, base + 2 * HEAD_DIM : base + 3 * HEAD_DIM]
        value = jnp.concatenate([value, minus], axis=1)
        scaled = grad_ref[:, cols].astype(f32) * inv_ref[:, cols]
        scaled_low = scaled.astype(bf16)
        inner = jnp.sum(scaled * mixed_ref[:, cols].astype(f32), axis=1, keepdims=True)
        inner_high = inner.astype(bf16).astype(f32)
        inner_pair = jnp.where(
            lane == 0, inner_high, jnp.where(lane == 1, inner - inner_high, 0.0)
        ).astype(bf16)
        wide = jnp.concatenate([scaled_low, inner_pair], axis=1)
        grad_key = grad_value = None
        for start in range(0, count, chunk):
            rows = slice(start, start + chunk)
            exponent = exp_ref[head, rows, :]
            grad_probs = mm(wide[rows], value, NT)
            grad_scores = (exponent.astype(f32) * grad_probs).astype(bf16)
            out_ref[rows, base : base + HEAD_DIM] = (mm(grad_scores, key) * scale).astype(bf16)
            key_part = mm(query[rows], grad_scores, TN)
            value_part = mm(scaled_low[rows], exponent, TN)
            grad_key = key_part if grad_key is None else grad_key + key_part
            grad_value = value_part if grad_value is None else grad_value + value_part
        out_ref[:, base + HEAD_DIM : base + 2 * HEAD_DIM] = (grad_key.T * scale).astype(bf16)
        out_ref[:, base + 2 * HEAD_DIM : base + 3 * HEAD_DIM] = grad_value.T.astype(bf16)


def attend_back(qkv, exponent, mixed, inverse, grad_mixed):
    count, width = qkv.shape
    pairs = width // (6 * HEAD_DIM)
    return pl.pallas_call(
        functools.partial(attend_back_kernel, min(512, count)),
        grid=(pairs,),
        in_specs=[
            pl.BlockSpec((count, 6 * HEAD_DIM), lambda p: (0, p)),
            pl.BlockSpec((2, count, count), lambda p: (p, 0, 0)),
        ]
        + [pl.BlockSpec((count, 2 * HEAD_DIM), lambda p: (0, p))] * 3,
        out_specs=pl.BlockSpec((count, 6 * HEAD_DIM), lambda p: (0, p)),
        out_shape=jax.ShapeDtypeStruct((count, width), bf16),
        compiler_params=pltpu.CompilerParams(vmem_limit_bytes=48 * 2**20),
        cost_estimate=QUICK,
        name="attend_back",
    )(qkv, exponent, mixed, inverse, grad_mixed)


def centre(values):
    centered = values - jnp.mean(values, axis=-1, keepdims=True)
    inverse = lax.rsqrt(jnp.mean(centered * centered, axis=-1, keepdims=True) + epsilon)
    return centered * inverse, inverse


def centre_back(grad, normed, inverse):
    return inverse * (
        grad
        - jnp.mean(grad, axis=-1, keepdims=True)
        - normed * jnp.mean(grad * normed, axis=-1, keepdims=True)
    )


def keep_sums(sums_ref, *values):
    @pl.when(pl.program_id(0) == 0)
    def _():
        sums_ref[...] = jnp.zeros_like(sums_ref)

    for i, value in enumerate(values):
        sums_ref[i : i + 1, :] += jnp.sum(value, axis=0, keepdims=True)


def norm_one_kernel(flags, vec_ref, tokens_ref, own_ref, arrived_ref, normed_ref, inv_ref, first_ref, low_ref):
    values = tokens_ref[...].astype(f32) + own_ref[...] + arrived_ref[...].astype(f32) + vec_ref[0:1, :]
    normed, inverse = centre(values)
    first = normed * vec_ref[1:2, :] + vec_ref[2:3, :]
    normed_ref[...] = normed
    inv_ref[...] = jnp.broadcast_to(inverse, inv_ref.shape)
    first_ref[...] = first
    low_ref[...] = first.astype(bf16)


def norm_two_kernel(
    flags, vec_ref, first_ref, own_ref, arrived_ref, cot_ref, keep_ref, give_ref, grad_ref, low_ref, sums_ref
):
    core = flags[1]
    values = first_ref[...] + own_ref[...] + arrived_ref[...].astype(f32) + vec_ref[3:4, :]
    normed, inverse = centre(values)
    output = (normed * vec_ref[4:5, :] + vec_ref[5:6, :]).astype(bf16)
    width = output.shape[1] // 4
    for part in range(2):
        even = output[:, 2 * part * width : (2 * part + 1) * width]
        odd = output[:, (2 * part + 1) * width : (2 * part + 2) * width]
        cols = slice(part * width, (part + 1) * width)
        keep_ref[:, cols] = jnp.where(core == 0, even, odd)
        give_ref[:, cols] = jnp.where(core == 0, odd, even)
    cot = cot_ref[...].astype(f32)
    grad = centre_back(cot * vec_ref[4:5, :], normed, inverse)
    low = grad.astype(bf16)
    grad_ref[...] = grad
    low_ref[...] = low
    keep_sums(sums_ref, cot * normed, cot, low.astype(f32))


def norm_back_kernel(
    flags, vec_ref, above_ref, own_ref, arrived_ref, normed_ref, inv_ref, grad_ref, low_ref, sums_ref
):
    normed = normed_ref[...]
    above = above_ref[...] + own_ref[...] + arrived_ref[...].astype(f32)
    grad = centre_back(above * vec_ref[1:2, :], normed, inv_ref[:, :1])
    low = grad.astype(bf16)
    grad_ref[...] = grad
    low_ref[...] = low
    keep_sums(sums_ref, above * normed, above, low.astype(f32))


def by_rows(kernel, flags, vec, operands, outs, name):
    rows, model = operands[1].shape
    tile = min(128, rows)

    def spec(width):
        return pl.BlockSpec((tile, width), lambda i, f: (i, 0))

    shapes = [
        jax.ShapeDtypeStruct((rows, width) if width else (8, model), dtype) for width, dtype in outs
    ]
    return pl.pallas_call(
        kernel,
        grid_spec=pltpu.PrefetchScalarGridSpec(
            num_scalar_prefetch=1,
            grid=(rows // tile,),
            in_specs=[pl.BlockSpec(vec.shape, lambda i, f: (0, 0))] + [spec(o.shape[1]) for o in operands],
            out_specs=[
                spec(width) if width else pl.BlockSpec((8, model), lambda i, f: (0, 0))
                for width, _ in outs
            ],
        ),
        out_shape=shapes,
        compiler_params=pltpu.CompilerParams(vmem_limit_bytes=40 * 2**20),
        cost_estimate=QUICK,
        name=name,
    )(flags, vec, *operands)


def feed_kernel(wide_ref, left_ref, right_ref, bias_ref, act_ref, slope_ref):
    side = left_ref.shape[0]
    pre = mm(wide_ref[:, :side], left_ref[...]) + mm(wide_ref[:, side:], right_ref[...]) + bias_ref[...]
    cdf = 0.5 * (1.0 + lax.erf(pre * (1.0 / math.sqrt(2.0))))
    pdf = jnp.exp(-0.5 * pre * pre) * (1.0 / math.sqrt(2.0 * math.pi))
    act_ref[...] = (pre * cdf).astype(bf16)
    slope_ref[...] = (cdf + pre * pdf).astype(bf16)


def feed(wide, left, right, bias):
    count, model = wide.shape
    side, width = left.shape
    tile = min(256, width)
    cols = lambda rows: pl.BlockSpec((rows, tile), lambda i: (0, i))
    return pl.pallas_call(
        feed_kernel,
        grid=(width // tile,),
        in_specs=[pl.BlockSpec((count, model), lambda i: (0, 0)), cols(side), cols(side), cols(1)],
        out_specs=[cols(count), cols(count)],
        out_shape=[jax.ShapeDtypeStruct((count, width), bf16)] * 2,
        compiler_params=pltpu.CompilerParams(vmem_limit_bytes=40 * 2**20),
        cost_estimate=QUICK,
        name="feed",
    )(wide, left, right, bias.reshape(1, width))


def feed_back_kernel(grad_ref, left_ref, right_ref, slope_ref, out_ref, sums_ref):
    side = left_ref.shape[1]
    product = mm(grad_ref[:, :side], left_ref[...], NT) + mm(grad_ref[:, side:], right_ref[...], NT)
    low = (product * slope_ref[...].astype(f32)).astype(bf16)
    out_ref[...] = low
    sums_ref[...] = jnp.sum(low.astype(f32), axis=0, keepdims=True)


def feed_back(grad, left, right, slope):
    count, model = grad.shape
    width, side = left.shape
    tile = min(256, width)
    cols = lambda rows: pl.BlockSpec((rows, tile), lambda i: (0, i))
    rows = pl.BlockSpec((tile, side), lambda i: (i, 0))
    return pl.pallas_call(
        feed_back_kernel,
        grid=(width // tile,),
        in_specs=[pl.BlockSpec((count, model), lambda i: (0, 0)), rows, rows, cols(count)],
        out_specs=[cols(count), cols(1)],
        out_shape=[jax.ShapeDtypeStruct((count, width), bf16), jax.ShapeDtypeStruct((1, width), f32)],
        compiler_params=pltpu.CompilerParams(vmem_limit_bytes=40 * 2**20),
        cost_estimate=QUICK,
        name="feed_back",
    )(grad, left, right, slope)


def weight_kernel(other_ref, mine_ref, right_ref, away_ref, own_ref, other_out, mine_out):
    step, part = pl.program_id(0), pl.num_programs(0) // 4
    side = own_ref.shape[1]

    def product(ref):
        return mm(ref[...], right_ref[...], TN).astype(bf16)

    def split(ref):
        value = product(ref)
        own_ref[...] = value[:, :side]
        away_ref[...] = value[:, side:]

    @pl.when(step < part)
    def _():
        split(other_ref)

    @pl.when((step >= part) & (step < 2 * part))
    def _():
        other_out[...] = product(other_ref)

    @pl.when((step >= 2 * part) & (step < 3 * part))
    def _():
        split(mine_ref)

    @pl.when(step >= 3 * part)
    def _():
        mine_out[...] = product(mine_ref)


def weight_grads(other, mine, right):
    count, width = other.shape
    model = right.shape[1]
    side = model // 2
    tile = min(256, width // 2)
    n = width // tile
    p = n // 2

    def stacked(i):
        return jnp.where(i < p, i, jnp.where(i < 2 * p, p - 1, jnp.minimum(i - p, 2 * p - 1)))

    return pl.pallas_call(
        weight_kernel,
        grid=(2 * n,),
        in_specs=[
            pl.BlockSpec((count, tile), lambda i: (0, jnp.minimum(i, n - 1))),
            pl.BlockSpec((count, tile), lambda i: (0, jnp.maximum(i - n, 0))),
            pl.BlockSpec((count, model), lambda i: (0, 0)),
        ],
        out_specs=[
            pl.BlockSpec((tile, side), lambda i: (stacked(i), 0)),
            pl.BlockSpec((tile, side), lambda i: (stacked(i), 0)),
            pl.BlockSpec((tile, model), lambda i: (jnp.clip(i - p, 0, p - 1), 0)),
            pl.BlockSpec((tile, model), lambda i: (jnp.clip(i - 3 * p, 0, p - 1), 0)),
        ],
        out_shape=[jax.ShapeDtypeStruct((width, side), bf16)] * 2
        + [jax.ShapeDtypeStruct((width // 2, model), bf16)] * 2,
        compiler_params=pltpu.CompilerParams(vmem_limit_bytes=40 * 2**20),
        cost_estimate=QUICK,
        name="weight_grads",
    )(other, mine, right)


def transposed_kernel(left_ref, right_ref, out_ref):
    out_ref[...] = mm(left_ref[...], right_ref[...], TN).astype(bf16)


def transposed(left, right):
    count, width = left.shape
    model = right.shape[1]
    tile = 384 if width % 384 == 0 else min(256, width)
    return pl.pallas_call(
        transposed_kernel,
        grid=(width // tile,),
        in_specs=[
            pl.BlockSpec((count, tile), lambda i: (0, i)), pl.BlockSpec((count, model), lambda i: (0, 0))
        ],
        out_specs=pl.BlockSpec((tile, model), lambda i: (i, 0)),
        out_shape=jax.ShapeDtypeStruct((width, model), bf16),
        compiler_params=pltpu.CompilerParams(vmem_limit_bytes=40 * 2**20),
        cost_estimate=QUICK,
        name="transposed",
    )(left, right)


def placed(kernel, flags, operands, shapes, name):
    return pl.pallas_call(
        kernel,
        grid_spec=pltpu.PrefetchScalarGridSpec(
            num_scalar_prefetch=1,
            grid=(1,),
            in_specs=[pl.BlockSpec(o.shape, lambda i, f, n=o.ndim: (0,) * n) for o in operands],
            out_specs=[pl.BlockSpec(s.shape, lambda i, f, n=len(s.shape): (0,) * n) for s in shapes],
        ),
        out_shape=shapes,
        compiler_params=pltpu.CompilerParams(vmem_limit_bytes=40 * 2**20),
        cost_estimate=QUICK,
        name=name,
    )(flags, *operands)


def block(index, size):
    return pl.ds(pl.multiple_of(index * size, size), size)


def join_wide_kernel(flags, mine_ref, near_ref, core_mine_ref, core_near_ref, out_ref):
    chip, core, place = flags[0], flags[1], flags[2]
    width, half = near_ref.shape[1], near_ref.shape[0] // 2
    own, away = block(core, half), block(1 - core, half)
    mine_at, near_at = 2 * place, 2 * (1 - place)
    for at, ref in ((mine_at + 1 - core, core_mine_ref), (near_at + core, near_ref), (near_at + 1 - core, core_near_ref)):
        out_ref[:half, block(at, width)] = ref[own, :]
        out_ref[half:, block(at, width)] = ref[away, :]
    out_ref[:half, block(mine_at + core, width)] = mine_ref[chip, own, :]
    out_ref[half:, block(mine_at + core, width)] = mine_ref[chip, away, :]


def give_core_kernel(flags, mine_ref, near_ref, out_ref):
    chip, core = flags[0], flags[1]
    width, half = near_ref.shape[1], near_ref.shape[0] // 2
    away = block(1 - core, half)
    out_ref[:, :width] = mine_ref[chip, away, :]
    out_ref[:, width:] = near_ref[away, :]


def join_own_kernel(flags, mine_ref, near_ref, core_ref, out_ref):
    chip, core, place = flags[0], flags[1], flags[2]
    width, half = near_ref.shape[1], near_ref.shape[0] // 2
    own = block(core, half)
    mine_at, near_at = 2 * place, 2 * (1 - place)
    out_ref[:, block(mine_at + core, width)] = mine_ref[chip, own, :]
    out_ref[:, block(near_at + core, width)] = near_ref[own, :]
    out_ref[:, block(mine_at + 1 - core, width)] = core_ref[:, :width]
    out_ref[:, block(near_at + 1 - core, width)] = core_ref[:, width:]


def split_core_kernel(flags, in_ref, keep_ref, send_ref):
    core = flags[1]
    width = in_ref.shape[1] // 4
    for part in range(2):
        cols = slice(part * width, (part + 1) * width)
        keep_ref[:, cols] = in_ref[:, block(2 * part + core, width)].astype(keep_ref.dtype)
        send_ref[:, cols] = in_ref[:, block(2 * part + 1 - core, width)].astype(send_ref.dtype)


def split_chip_kernel(flags, own_ref, away_ref, keep_ref, send_ref):
    core, place = flags[1], flags[2]
    half, width = own_ref.shape[0], own_ref.shape[1] // 2
    for rows, ref in ((block(core, half), own_ref), (block(1 - core, half), away_ref)):
        keep_ref[rows, :] = ref[:, block(place, width)]
        send_ref[rows, :] = ref[:, block(1 - place, width)]


def add_split_chip_kernel(flags, here_ref, there_ref, keep_ref, send_ref):
    core, place = flags[1], flags[2]
    half, width = here_ref.shape[0] // 2, here_ref.shape[1] // 2
    for rows, here, there in (
        (block(core, half), slice(0, half), slice(half, None)),
        (block(1 - core, half), slice(half, None), slice(0, half)),
    ):
        for ref, at in ((keep_ref, place), (send_ref, 1 - place)):
            cols = block(at, width)
            ref[rows, :] = (here_ref[here, cols] + there_ref[there, cols].astype(f32)).astype(bf16)


def join_sequences_kernel(flags, keep_ref, near_ref, out_ref):
    chip = flags[0]
    out_ref[chip] = keep_ref[...]
    out_ref[1 - chip] = near_ref[...]


def pick(values, index, axis=0):
    return lax.dynamic_index_in_dim(values, index, axis, keepdims=False)


def after(values, *others):
    return lax.optimization_barrier((values, *others))[0]


def hold(values, *arrived):
    return lax.optimization_barrier((values, *arrived))


def added(own, arrived):
    return (own.astype(f32) + arrived.astype(f32)).astype(bf16)


class PairSum:
    def __init__(self, values):
        self.values = values
        self.size = lax.axis_size("dp")
        self.index = lax.axis_index("dp")
        self.undo = []
        self.todo = []
        rows, bit = values.shape[0], 1
        while self.size & (self.size - 1) == 0 and bit < self.size and rows % 32 == 0:
            self.todo.append(("halve", bit))
            rows, bit = rows // 2, bit * 2
        if bit < self.size:
            self.todo.append(("rest", bit))
        self.todo += [("double", b) for kind, b in reversed(self.todo) if kind == "halve"]

    def send(self):
        kind, bit = self.todo[0]
        pairs = [(i, i ^ bit) for i in range(self.size)]
        upper = (self.index & bit) != 0
        if kind == "halve":
            rows = self.values.shape[0] // 2
            low, high = self.values[:rows], self.values[rows:]
            self.values, give = jnp.where(upper, high, low), jnp.where(upper, low, high)
            self.arrived = lax.ppermute(give, "dp", pairs)
        elif kind == "double":
            self.arrived = lax.ppermute(self.values, "dp", pairs)
        else:
            groups = [[i + bit * j for j in range(self.size // bit)] for i in range(bit)]
            self.arrived = lax.psum(self.values, "dp", axis_index_groups=groups)

    def receive(self):
        kind, bit = self.todo.pop(0)
        upper = (self.index & bit) != 0
        if kind == "halve":
            self.values = added(self.values, self.arrived)
        elif kind == "double":
            pair = (self.arrived, self.values), (self.values, self.arrived)
            self.values = jnp.where(upper, jnp.concatenate(pair[0]), jnp.concatenate(pair[1]))
        else:
            self.values = self.arrived

    def step(self, *others):
        if not self.todo:
            return others
        self.arrived, *others = hold(self.arrived, *others)
        self.receive()
        if self.todo:
            self.send()
        return others

    def finish(self):
        while self.todo:
            self.step()
        return self.values


def body(
    tokens, segments, w_qkv, qv_bias, w_out, out_bias, gain_one, shift_one,
    w_in, in_bias, w_down, down_bias, gain_two, shift_two, cotangent,
):
    row = lax.axis_index("row")
    col = lax.axis_index("col")
    chip, core = col // 2, col % 2
    same = row == chip
    first_core = core == 0
    flags = jnp.stack([chip, core, jnp.where(same, 0, 1)]).astype(jnp.int32)
    seq_count, count, width = tokens.shape
    half = count // 2
    model = width * lax.axis_size("col")
    heads = qv_bias.shape[0] // (2 * HEAD_DIM)
    hidden = in_bias.shape[0]
    cut, mid = 3 * heads * HEAD_DIM // 2, hidden // 2

    def shape(*dims, dtype=bf16):
        return jax.ShapeDtypeStruct(dims, dtype)

    qv_pairs = qv_bias.reshape(heads, 2, HEAD_DIM)
    qkv_bias = jnp.stack(
        [qv_pairs[:, 0], jnp.zeros_like(qv_pairs[:, 0]), qv_pairs[:, 1]], axis=1
    ).reshape(-1)
    vectors = jnp.concatenate([out_bias, gain_one, shift_one, down_bias, gain_two, shift_two])
    small = jnp.concatenate([vectors, qkv_bias, in_bias])
    small_near = to_chip(small)

    near = to_chip(pick(tokens, 1 - chip))
    qkv_row = to_row(w_qkv)
    core_mine = to_core(pick(tokens, chip))
    core_near = to_core(near)
    wide = placed(
        join_wide_kernel, flags, [tokens, near, core_mine, core_near], [shape(count, model)], "join_wide"
    )[0]

    segment = pick(segments, chip).reshape(2, half)
    segment = jnp.concatenate([pick(segment, core), pick(segment, 1 - core)])
    ids = jnp.arange(HEAD_DIM)
    differs = jnp.where((segment[:, None] != ids) & (ids < 3), -(2.0**30), 0.0)
    mask = jnp.concatenate([differs, segment[:, None] == ids], axis=1).astype(bf16)

    qkv_own = after(w_qkv, near)
    near_a, near_b = to_chip(qkv_own[:, :cut]), to_chip(qkv_own[:, cut:])
    far_a = to_row(near_a)
    wide, small_near, qkv_row = hold(wide, small_near, qkv_row)
    far_b = to_chip(qkv_row[:, cut:])
    out_row = to_row(after(w_out, wide))
    in_row = to_row(after(w_in, wide))
    mine = attend(wide, w_qkv, qkv_row, qkv_bias, mask)
    qkv_bias_near = small_near[6 * width : 6 * width + 2 * cut]
    wide_a, near_b, far_a, far_b, out_row = hold(after(wide, mine[0]), near_b, far_a, far_b, out_row)
    out_near = to_chip(after(w_out, out_row))
    out_far = to_chip(out_row)
    in_near = to_chip(after(w_in, out_row))
    down_row = to_row(after(w_down, out_row))
    other_a = attend(wide_a, near_a, far_a, qkv_bias_near[:cut], mask)
    wide_b, out_near, out_far, in_row = hold(after(wide, other_a[0]), out_near, out_far, in_row)
    down_near = to_chip(after(w_down, out_near))
    other_b = attend(wide_b, near_b, far_b, qkv_bias_near[cut:], mask)
    parts = [mine, other_a, other_b]
    lefts = [w_qkv, near_a, near_b]
    rights = [qkv_row, far_a, far_b]
    mixed = [mine[2], jnp.concatenate([other_a[2], other_b[2]], axis=1)]
    w_outs = [
        jnp.concatenate([w_out, out_row], axis=1), jnp.concatenate([out_near, out_far], axis=1)
    ]

    vec = vectors.reshape(6, width)
    vec_near = small_near[: 6 * width].reshape(6, width)
    low, high = jnp.where(same, vec, vec_near), jnp.where(same, vec_near, vec)
    both = jnp.concatenate([low, high], axis=1)
    there = to_core(after(both, mine[0]))
    even, odd = jnp.where(first_core, both, there), jnp.where(first_core, there, both)
    wide_vec = jnp.concatenate(
        [even[:, :width], odd[:, :width], even[:, width:], odd[:, width:]], axis=1
    )
    wide_vec = jnp.concatenate([wide_vec, jnp.zeros((2, model), f32)], axis=0)
    in_biases = [in_bias, small_near[6 * width + 2 * cut :]]

    def core_gather(values):
        return jnp.concatenate([values, to_core(values)], axis=0)

    arrived = to_core(sum(mm(m[half:], w) for m, w in zip(mixed, w_outs)).astype(bf16))
    own = sum(mm(m[:half], w) for m, w in zip(mixed, w_outs))
    normed_one, inverse_one, first_out, first_low = by_rows(
        norm_one_kernel, flags, wide_vec, [wide[:half], own, arrived],
        [(model, f32), (128, f32), (model, f32), (model, bf16)], "norm_one",
    )
    first_wide = core_gather(first_low)

    first_wide, in_near = hold(first_wide, in_near)
    in_far = to_row(in_near)
    act_mine, slope_mine = feed(first_wide, w_in, in_row, in_biases[0])
    down_mine = jnp.concatenate([w_down, down_row], axis=1)
    down_far_a = to_chip(down_row[:mid])
    ffn_mine = [mm(act_mine[half:], down_mine), mm(act_mine[:half], down_mine)]
    cot_near = to_chip(after(pick(cotangent, 1 - chip), down_row))
    down_near, *ffn_mine = hold(down_near, *ffn_mine)
    down_far_b = to_row(down_near[mid:])
    act_other, slope_other = feed(after(first_wide, down_near), in_near, in_far, in_biases[1])
    down_far = jnp.concatenate([down_far_a, down_far_b], axis=0)
    down_other = jnp.concatenate([down_near, down_far], axis=1)
    arrived = to_core((ffn_mine[0] + mm(act_other[half:], down_other)).astype(bf16))
    own = ffn_mine[1] + mm(act_other[:half], down_other)
    cot_give = placed(give_core_kernel, flags, [cotangent, cot_near], [shape(half, 2 * width)], "give_core")[0]
    cot_core = to_core(cot_give)
    cot = placed(
        join_own_kernel, flags, [cotangent, cot_near, cot_core], [shape(half, model)], "join_own"
    )[0]
    out_keep, out_give, grad_pre_two, grad_ffn, sums_two = by_rows(
        norm_two_kernel, flags, wide_vec, [first_out, own, arrived, cot],
        [(2 * width, bf16), (2 * width, bf16), (model, f32), (model, bf16), (0, f32)], "norm_two",
    )

    side = model // 2

    def second_sends(own_a, arrived_a, mine_b, arrived_b):
        size = own_a.shape[0] // 2
        sum_a, sum_b = added(own_a, arrived_a), added(mine_b, arrived_b)
        return (sum_a[size:], to_chip(sum_a[:size])), (sum_b[:, :side], to_row(sum_b[:, side:]))

    gw = core_gather(grad_ffn)
    down_away_a, down_own_a, down_other_b, down_mine_b = weight_grads(act_other, act_mine, gw)
    down_first = [to_row(down_away_a), to_chip(down_other_b)]
    hid_mine, in_sum_mine = feed_back(gw, w_down, down_row, slope_mine)
    hid_other, in_sum_other = feed_back(gw, down_near, down_far, slope_other)
    grad_in_biases = [in_sum_mine[0], in_sum_other[0]]
    in_mine = jnp.concatenate([w_in, in_row], axis=0)
    in_other = jnp.concatenate([in_near, in_far], axis=0)
    arrived = to_core((mm(hid_mine[half:], in_mine, NT) + mm(hid_other[half:], in_other, NT)).astype(bf16))
    own = mm(hid_mine[:half], in_mine, NT) + mm(hid_other[:half], in_other, NT)
    in_away_a, in_own_a, in_other_b, in_mine_b = weight_grads(hid_other, hid_mine, first_wide)
    own, arrived, *down_first = hold(own, arrived, *down_first)
    (da, da_near), (db, db_row) = second_sends(down_own_a, down_first[0], down_mine_b, down_first[1])
    in_first = [to_row(after(in_away_a, da)), to_chip(after(in_other_b, db))]

    grad_pre_one, grad_attention, sums_one = by_rows(
        norm_back_kernel, flags, wide_vec, [grad_pre_two, own, arrived, normed_one, inverse_one],
        [(model, f32), (model, bf16), (0, f32)], "norm_back",
    )
    grad_attn_wide = core_gather(grad_attention)
    grad_mixed = [mm(grad_attn_wide, w, NT).astype(bf16) for w in w_outs[::-1]][::-1]
    narrow = grad_mixed[1].shape[1] // 2
    grad_outs = [transposed(m, grad_attn_wide) for m in mixed]
    grad_outs[0], grad_outs[1], grad_mixed[1], da_near, db_row = hold(*grad_outs, grad_mixed[1], da_near, db_row)
    sum_down = PairSum(jnp.concatenate([added(da, da_near), added(db, db_row)], axis=0))
    sum_down.send()
    go_a = attend_back(*other_a, after(grad_mixed[1][:, :narrow], sum_down.values))
    wt_oa = transposed(go_a, wide)
    go_b = attend_back(*other_b, after(grad_mixed[1][:, narrow:], go_a))
    wt_ob = transposed(go_b, wide)
    (gm, go_b, wt_oa, wt_ob, *in_first) = sum_down.step(grad_mixed[0], go_b, wt_oa, wt_ob, *in_first)
    (ia, ia_near), (ib, ib_row) = second_sends(in_own_a, in_first[0], in_mine_b, in_first[1])
    qkv_a_other = to_row(after(wt_oa[:, side:], ib))
    go_m = attend_back(*mine, after(gm, ia, ib))
    out_row_grads = to_row(jnp.concatenate([g[:, side:] for g in grad_outs[::-1]], axis=0))
    go_m, ia_near, ib_row = sum_down.step(go_m, ia_near, ib_row)
    grad_mine = go_m
    sum_in = PairSum(jnp.concatenate([added(ia, ia_near), added(ib, ib_row)], axis=0))
    sum_in.send()
    wt_m = transposed(grad_mine, wide)
    qkv_a_mine = to_row(wt_m[:cut, side:])
    rows = grad_outs[0].shape[0]
    out_sums = added(
        jnp.concatenate([g[:, :side] for g in grad_outs[::-1]], axis=0), out_row_grads
    )
    out_near_grad = to_chip(out_sums[:rows])

    features = jnp.concatenate([sums_one[2:3], sums_one[:2], sums_two[2:3], sums_two[:2]], axis=0)
    f0, f1, f2, f3 = [features[:, i * width : (i + 1) * width] for i in range(4)]
    keep = jnp.concatenate([jnp.where(first_core, f0, f1), jnp.where(first_core, f2, f3)], axis=1)
    give = jnp.concatenate([jnp.where(first_core, f1, f0), jnp.where(first_core, f3, f2)], axis=1)
    features = keep + to_core(give)
    feature_mine = jnp.where(same, features[:, :width], features[:, width:])
    feature_near = jnp.where(same, features[:, width:], features[:, :width])
    extras = []
    for g, i, f in zip(((grad_mine,), (go_a, go_b)), grad_in_biases, (feature_mine, feature_near)):
        sums = jnp.concatenate([jnp.sum(v, axis=0, dtype=f32) for v in g]).reshape(heads, 3, HEAD_DIM)
        sums = jnp.stack([sums[:, 0], sums[:, 2]], axis=1).reshape(-1)
        flat = jnp.concatenate([sums, i, f.reshape(-1)])
        lines = -(-flat.shape[0] // (64 * side)) * 64
        flat = jnp.pad(flat, (0, lines * side - flat.shape[0])).reshape(lines, side).astype(bf16)
        extras.append(jnp.concatenate([flat, flat], axis=1))

    b_near = to_chip(jnp.concatenate([wt_ob, extras[1]], axis=0))
    sum_mine = added(wt_m[:cut, :side], qkv_a_mine)
    a_near = to_chip(added(wt_oa[:, :side], qkv_a_other))
    sum_b = added(jnp.concatenate([wt_m[cut:], extras[0]], axis=0), b_near)
    b_row = to_row(sum_b[:, side:])
    grads = [grad_mine, go_a, go_b]
    grad_left, grad_right = [sum(mm(g, w, NT) for g, w in zip(grads, ws)) for ws in (lefts, rights)]
    grad_left, grad_right = sum_down.step(grad_left, grad_right)
    sum_in.step()
    sum_qkv = PairSum(
        jnp.concatenate(
            [added(sum_mine, a_near), added(sum_b[:, :side], b_row), added(out_sums[rows:], out_near_grad)], axis=0
        )
    )
    sum_qkv.send()
    sum_down.step()
    for _ in range(8):
        sum_qkv.step()
        sum_in.step()
    grad_w_down = sum_down.finish()
    grad_w_in = sum_in.finish()
    summed = sum_qkv.finish().astype(f32)
    grad_w_qkv = summed[: 2 * cut].T
    part_b = summed[2 * cut : -rows]
    grad_w_out = summed[-rows:]
    small = part_b.reshape(-1)
    qv_len = qv_bias.shape[0]
    g_qv, g_in = small[:qv_len], small[qv_len : qv_len + hidden]
    g_out, g_gone, g_sone, g_down, g_gtwo, g_stwo = small[
        qv_len + hidden : qv_len + hidden + 6 * width
    ].reshape(6, width)

    grad_wide = jnp.concatenate([grad_left, grad_right], axis=1)
    grad_wide = jnp.concatenate([grad_wide[:half] + grad_pre_one, grad_wide[half:]], axis=0)

    keep, give = placed(
        split_chip_kernel, flags, [out_keep, to_core(out_give)], [shape(count, width)] * 2, "split_chip"
    )
    output = placed(
        join_sequences_kernel, flags, [keep, to_chip(give)], [shape(2, count, width)], "join_sequences"
    )[0]
    keep, give = placed(
        split_core_kernel, flags, [grad_wide],
        [shape(count, 2 * width, dtype=f32), shape(count, 2 * width)], "split_core",
    )
    keep, give = placed(
        add_split_chip_kernel, flags, [keep, to_core(give)], [shape(count, width)] * 2, "add_split_chip"
    )
    grad_tokens = placed(
        join_sequences_kernel, flags, [keep, to_chip(give)], [shape(2, count, width)], "join_sequences"
    )[0]
    return (
        output, grad_tokens, grad_w_qkv, g_qv, grad_w_out, g_out, g_gone, g_sone,
        grad_w_in.astype(f32).T, g_in, grad_w_down.astype(f32), g_down, g_gtwo, g_stwo,
    )


def solution(mesh):
    tokens = P(("dp", "row"), None, "col")
    feature = P("col")
    by_row, by_col = P("row", "col"), P("col", "row")
    return jax.shard_map(
        body,
        mesh=mesh,
        in_specs=(
            tokens, P(("dp", "row"), None), by_row, feature, by_col, feature, feature, feature,
            by_row, feature, by_col, feature, feature, feature, tokens,
        ),
        out_specs=(
            tokens, tokens, by_row, feature, by_col, feature, feature, feature,
            by_row, feature, by_col, feature, feature, feature,
        ),
        check_vma=False,
    )
```

```python
import functools
import math

import jax
import jax.numpy as jnp
from jax import lax
from jax.experimental import pallas as pl
from jax.experimental.pallas import tpu as pltpu
from jax.sharding import PartitionSpec as P

HEAD_DIM = 64
epsilon = 1e-12
f32 = jnp.float32
bf16 = jnp.bfloat16
NT = (((1,), (1,)), ((), ()))
NN = (((1,), (0,)), ((), ()))
TN = (((0,), (0,)), ((), ()))


QUICK = pl.CostEstimate(flops=1024, bytes_accessed=1024, transcendentals=0)


def mm(left, right, dims=NN):
    return lax.dot_general(left, right, dims, preferred_element_type=f32)


def to_core(values):
    size = lax.axis_size("col")
    return lax.ppermute(values, "col", [(i, i ^ 1) for i in range(size)])


def to_chip(values):
    size = lax.axis_size("col")
    return lax.ppermute(values, "col", [(i, i ^ 2) for i in range(size)])


def to_row(values):
    return lax.ppermute(values, "row", [(0, 1), (1, 0)])


def attend_kernel(chunk, wide_ref, left_ref, right_ref, bias_ref, mask_ref, qkv_ref, exp_ref, mixed_ref, inv_ref):
    count, side = wide_ref.shape[0], left_ref.shape[0]
    projected = mm(wide_ref[:, :side], left_ref[...]) + mm(wide_ref[:, side:], right_ref[...])
    qkv_ref[...] = (projected + bias_ref[...]).astype(bf16)
    ones = jnp.ones((count, HEAD_DIM), bf16)
    for head in range(2):
        base = 3 * HEAD_DIM * head
        cols = slice(head * HEAD_DIM, (head + 1) * HEAD_DIM)
        query = qkv_ref[:, base : base + HEAD_DIM] * bf16(1.0 / math.sqrt(HEAD_DIM))
        key = qkv_ref[:, base + HEAD_DIM : base + 2 * HEAD_DIM]
        value = qkv_ref[:, base + 2 * HEAD_DIM : base + 3 * HEAD_DIM]
        query = jnp.concatenate([query, mask_ref[:, :HEAD_DIM]], axis=1)
        key = jnp.concatenate([key, mask_ref[:, HEAD_DIM:]], axis=1)
        value = jnp.concatenate([value, ones], axis=1)
        for start in range(0, count, chunk):
            rows = slice(start, start + chunk)
            scores = mm(query[rows], key, NT)
            top = jnp.max(scores, axis=-1, keepdims=True)
            exponent = jnp.exp(scores - top).astype(bf16)
            exp_ref[head, rows, :] = exponent
            mixed = mm(exponent, value)
            inverse = 1.0 / mixed[:, HEAD_DIM:]
            mixed_ref[rows, cols] = (mixed[:, :HEAD_DIM] * inverse).astype(bf16)
            inv_ref[rows, cols] = inverse


def attend(wide, left, right, bias, mask):
    count, model = wide.shape
    side, width = left.shape
    six = 6 * HEAD_DIM
    pairs = width // six
    return pl.pallas_call(
        functools.partial(attend_kernel, min(512, count)),
        grid=(pairs,),
        in_specs=[
            pl.BlockSpec((count, model), lambda p: (0, 0)),
            pl.BlockSpec((side, six), lambda p: (0, p)),
            pl.BlockSpec((side, six), lambda p: (0, p)),
            pl.BlockSpec((1, six), lambda p: (0, p)),
            pl.BlockSpec((count, 2 * HEAD_DIM), lambda p: (0, 0)),
        ],
        out_specs=[
            pl.BlockSpec((count, six), lambda p: (0, p)),
            pl.BlockSpec((2, count, count), lambda p: (p, 0, 0)),
            pl.BlockSpec((count, 2 * HEAD_DIM), lambda p: (0, p)),
            pl.BlockSpec((count, 2 * HEAD_DIM), lambda p: (0, p)),
        ],
        out_shape=[
            jax.ShapeDtypeStruct((count, width), bf16),
            jax.ShapeDtypeStruct((2 * pairs, count, count), bf16),
            jax.ShapeDtypeStruct((count, 2 * HEAD_DIM * pairs), bf16),
            jax.ShapeDtypeStruct((count, 2 * HEAD_DIM * pairs), f32),
        ],
        compiler_params=pltpu.CompilerParams(vmem_limit_bytes=52 * 2**20),
        cost_estimate=QUICK,
        name="attend",
    )(wide, left, right, bias.reshape(1, width), mask)


def attend_back_kernel(chunk, qkv_ref, exp_ref, mixed_ref, inv_ref, grad_ref, out_ref):
    count = qkv_ref.shape[0]
    lane = lax.broadcasted_iota(jnp.int32, (count, HEAD_DIM), 1)
    minus = jnp.where(lane < 2, -1.0, 0.0).astype(bf16)
    scale = 1.0 / math.sqrt(HEAD_DIM)
    for head in range(2):
        base = 3 * HEAD_DIM * head
        cols = slice(head * HEAD_DIM, (head + 1) * HEAD_DIM)
        query = qkv_ref[:, base : base + HEAD_DIM]
        key = qkv_ref[:, base + HEAD_DIM : base + 2 * HEAD_DIM]
        value = qkv_ref[:, base + 2 * HEAD_DIM : base + 3 * HEAD_DIM]
        value = jnp.concatenate([value, minus], axis=1)
        scaled = grad_ref[:, cols].astype(f32) * inv_ref[:, cols]
        scaled_low = scaled.astype(bf16)
        inner = jnp.sum(scaled * mixed_ref[:, cols].astype(f32), axis=1, keepdims=True)
        inner_high = inner.astype(bf16).astype(f32)
        inner_pair = jnp.where(
            lane == 0, inner_high, jnp.where(lane == 1, inner - inner_high, 0.0)
        ).astype(bf16)
        wide = jnp.concatenate([scaled_low, inner_pair], axis=1)
        grad_key = grad_value = None
        for start in range(0, count, chunk):
            rows = slice(start, start + chunk)
            exponent = exp_ref[head, rows, :]
            grad_probs = mm(wide[rows], value, NT)
            grad_scores = (exponent.astype(f32) * grad_probs).astype(bf16)
            out_ref[rows, base : base + HEAD_DIM] = (mm(grad_scores, key) * scale).astype(bf16)
            key_part = mm(query[rows], grad_scores, TN)
            value_part = mm(scaled_low[rows], exponent, TN)
            grad_key = key_part if grad_key is None else grad_key + key_part
            grad_value = value_part if grad_value is None else grad_value + value_part
        out_ref[:, base + HEAD_DIM : base + 2 * HEAD_DIM] = (grad_key.T * scale).astype(bf16)
        out_ref[:, base + 2 * HEAD_DIM : base + 3 * HEAD_DIM] = grad_value.T.astype(bf16)


def attend_back(qkv, exponent, mixed, inverse, grad_mixed, first=0, at=0):
    count, width = qkv.shape
    pairs, width = 1, 6 * HEAD_DIM
    return pl.pallas_call(
        functools.partial(attend_back_kernel, min(512, count)),
        grid=(pairs,),
        in_specs=[
            pl.BlockSpec((count, 6 * HEAD_DIM), lambda p: (0, p + first)),
            pl.BlockSpec((2, count, count), lambda p: (p + first, 0, 0)),
        ]
        + [pl.BlockSpec((count, 2 * HEAD_DIM), lambda p: (0, p + first))] * 2
        + [pl.BlockSpec((count, 2 * HEAD_DIM), lambda p: (0, p + at))],
        out_specs=pl.BlockSpec((count, 6 * HEAD_DIM), lambda p: (0, p)),
        out_shape=jax.ShapeDtypeStruct((count, width), bf16),
        compiler_params=pltpu.CompilerParams(vmem_limit_bytes=48 * 2**20),
        cost_estimate=QUICK,
        name="attend_back",
    )(qkv, exponent, mixed, inverse, grad_mixed)


def centre(values):
    centered = values - jnp.mean(values, axis=-1, keepdims=True)
    inverse = lax.rsqrt(jnp.mean(centered * centered, axis=-1, keepdims=True) + epsilon)
    return centered * inverse, inverse


def centre_back(grad, normed, inverse):
    return inverse * (
        grad
        - jnp.mean(grad, axis=-1, keepdims=True)
        - normed * jnp.mean(grad * normed, axis=-1, keepdims=True)
    )


def keep_sums(sums_ref, *values):
    @pl.when(pl.program_id(0) == 0)
    def _():
        sums_ref[...] = jnp.zeros_like(sums_ref)

    for i, value in enumerate(values):
        sums_ref[i : i + 1, :] += jnp.sum(value, axis=0, keepdims=True)


def norm_one_kernel(flags, vec_ref, tokens_ref, own_ref, arrived_ref, normed_ref, inv_ref, first_ref, low_ref):
    values = tokens_ref[...].astype(f32) + own_ref[...] + arrived_ref[...].astype(f32) + vec_ref[0:1, :]
    normed, inverse = centre(values)
    first = normed * vec_ref[1:2, :] + vec_ref[2:3, :]
    normed_ref[...] = normed
    inv_ref[...] = jnp.broadcast_to(inverse, inv_ref.shape)
    first_ref[...] = first
    low_ref[...] = first.astype(bf16)


def norm_two_kernel(
    flags, vec_ref, first_ref, own_ref, arrived_ref, cot_ref, keep_ref, give_ref, grad_ref, low_ref, sums_ref
):
    core = flags[1]
    values = first_ref[...] + own_ref[...] + arrived_ref[...].astype(f32) + vec_ref[3:4, :]
    normed, inverse = centre(values)
    output = (normed * vec_ref[4:5, :] + vec_ref[5:6, :]).astype(bf16)
    width = output.shape[1] // 4
    for part in range(2):
        even = output[:, 2 * part * width : (2 * part + 1) * width]
        odd = output[:, (2 * part + 1) * width : (2 * part + 2) * width]
        cols = slice(part * width, (part + 1) * width)
        keep_ref[:, cols] = jnp.where(core == 0, even, odd)
        give_ref[:, cols] = jnp.where(core == 0, odd, even)
    cot = cot_ref[...].astype(f32)
    grad = centre_back(cot * vec_ref[4:5, :], normed, inverse)
    low = grad.astype(bf16)
    grad_ref[...] = grad
    low_ref[...] = low
    keep_sums(sums_ref, cot * normed, cot, low.astype(f32))


def norm_back_kernel(
    flags, vec_ref, above_ref, own_ref, arrived_ref, normed_ref, inv_ref, grad_ref, low_ref, sums_ref
):
    normed = normed_ref[...]
    above = above_ref[...] + own_ref[...] + arrived_ref[...].astype(f32)
    grad = centre_back(above * vec_ref[1:2, :], normed, inv_ref[:, :1])
    low = grad.astype(bf16)
    grad_ref[...] = grad
    low_ref[...] = low
    keep_sums(sums_ref, above * normed, above, low.astype(f32))


def by_rows(kernel, flags, vec, operands, outs, name):
    rows, model = operands[1].shape
    tile = min(128, rows)

    def spec(width):
        return pl.BlockSpec((tile, width), lambda i, f: (i, 0))

    shapes = [
        jax.ShapeDtypeStruct((rows, width) if width else (8, model), dtype) for width, dtype in outs
    ]
    return pl.pallas_call(
        kernel,
        grid_spec=pltpu.PrefetchScalarGridSpec(
            num_scalar_prefetch=1,
            grid=(rows // tile,),
            in_specs=[pl.BlockSpec(vec.shape, lambda i, f: (0, 0))] + [spec(o.shape[1]) for o in operands],
            out_specs=[
                spec(width) if width else pl.BlockSpec((8, model), lambda i, f: (0, 0))
                for width, _ in outs
            ],
        ),
        out_shape=shapes,
        compiler_params=pltpu.CompilerParams(vmem_limit_bytes=40 * 2**20),
        cost_estimate=QUICK,
        name=name,
    )(flags, vec, *operands)


def feed_kernel(wide_ref, left_ref, right_ref, bias_ref, act_ref, slope_ref):
    side = left_ref.shape[0]
    pre = mm(wide_ref[:, :side], left_ref[...]) + mm(wide_ref[:, side:], right_ref[...]) + bias_ref[...]
    cdf = 0.5 * (1.0 + lax.erf(pre * (1.0 / math.sqrt(2.0))))
    pdf = jnp.exp(-0.5 * pre * pre) * (1.0 / math.sqrt(2.0 * math.pi))
    act_ref[...] = (pre * cdf).astype(bf16)
    slope_ref[...] = (cdf + pre * pdf).astype(bf16)


def feed(wide, left, right, bias):
    count, model = wide.shape
    side, width = left.shape
    tile = min(256, width)
    cols = lambda rows: pl.BlockSpec((rows, tile), lambda i: (0, i))
    return pl.pallas_call(
        feed_kernel,
        grid=(width // tile,),
        in_specs=[pl.BlockSpec((count, model), lambda i: (0, 0)), cols(side), cols(side), cols(1)],
        out_specs=[cols(count), cols(count)],
        out_shape=[jax.ShapeDtypeStruct((count, width), bf16)] * 2,
        compiler_params=pltpu.CompilerParams(vmem_limit_bytes=40 * 2**20),
        cost_estimate=QUICK,
        name="feed",
    )(wide, left, right, bias.reshape(1, width))


def feed_back_kernel(grad_ref, left_ref, right_ref, slope_ref, out_ref, sums_ref):
    side = left_ref.shape[1]
    product = mm(grad_ref[:, :side], left_ref[...], NT) + mm(grad_ref[:, side:], right_ref[...], NT)
    low = (product * slope_ref[...].astype(f32)).astype(bf16)
    out_ref[...] = low
    sums_ref[...] = jnp.sum(low.astype(f32), axis=0, keepdims=True)


def feed_back(grad, left, right, slope):
    count, model = grad.shape
    width, side = left.shape
    tile = min(256, width)
    cols = lambda rows: pl.BlockSpec((rows, tile), lambda i: (0, i))
    rows = pl.BlockSpec((tile, side), lambda i: (i, 0))
    return pl.pallas_call(
        feed_back_kernel,
        grid=(width // tile,),
        in_specs=[pl.BlockSpec((count, model), lambda i: (0, 0)), rows, rows, cols(count)],
        out_specs=[cols(count), cols(1)],
        out_shape=[jax.ShapeDtypeStruct((count, width), bf16), jax.ShapeDtypeStruct((1, width), f32)],
        compiler_params=pltpu.CompilerParams(vmem_limit_bytes=40 * 2**20),
        cost_estimate=QUICK,
        name="feed_back",
    )(grad, left, right, slope)


def weight_kernel(other_ref, mine_ref, right_ref, away_ref, own_ref, other_out, mine_out):
    step, part = pl.program_id(0), pl.num_programs(0) // 4
    side = own_ref.shape[1]

    def product(ref):
        return mm(ref[...], right_ref[...], TN).astype(bf16)

    def split(ref):
        value = product(ref)
        own_ref[...] = value[:, :side]
        away_ref[...] = value[:, side:]

    @pl.when(step < part)
    def _():
        split(other_ref)

    @pl.when((step >= part) & (step < 2 * part))
    def _():
        other_out[...] = product(other_ref)

    @pl.when((step >= 2 * part) & (step < 3 * part))
    def _():
        split(mine_ref)

    @pl.when(step >= 3 * part)
    def _():
        mine_out[...] = product(mine_ref)


def weight_grads(other, mine, right):
    count, width = other.shape
    model = right.shape[1]
    side = model // 2
    tile = min(256, width // 2)
    n = width // tile
    p = n // 2

    def stacked(i):
        return jnp.where(i < p, i, jnp.where(i < 2 * p, p - 1, jnp.minimum(i - p, 2 * p - 1)))

    return pl.pallas_call(
        weight_kernel,
        grid=(2 * n,),
        in_specs=[
            pl.BlockSpec((count, tile), lambda i: (0, jnp.minimum(i, n - 1))),
            pl.BlockSpec((count, tile), lambda i: (0, jnp.maximum(i - n, 0))),
            pl.BlockSpec((count, model), lambda i: (0, 0)),
        ],
        out_specs=[
            pl.BlockSpec((tile, side), lambda i: (stacked(i), 0)),
            pl.BlockSpec((tile, side), lambda i: (stacked(i), 0)),
            pl.BlockSpec((tile, model), lambda i: (jnp.clip(i - p, 0, p - 1), 0)),
            pl.BlockSpec((tile, model), lambda i: (jnp.clip(i - 3 * p, 0, p - 1), 0)),
        ],
        out_shape=[jax.ShapeDtypeStruct((width, side), bf16)] * 2
        + [jax.ShapeDtypeStruct((width // 2, model), bf16)] * 2,
        compiler_params=pltpu.CompilerParams(vmem_limit_bytes=40 * 2**20),
        cost_estimate=QUICK,
        name="weight_grads",
    )(other, mine, right)


def second_kernel(own_a, arrived_a, mine_b, arrived_b, a_other, a_mine, b_own, b_away):
    size, side = a_mine.shape

    def added(x, y):
        return (x.astype(f32) + y.astype(f32)).astype(bf16)

    a_other[...] = added(own_a[:size], arrived_a[:size])
    a_mine[...] = added(own_a[size:], arrived_a[size:])
    b_own[...] = added(mine_b[:, :side], arrived_b[:, :side])
    b_away[...] = added(mine_b[:, side:], arrived_b[:, side:])


def joined_kernel(a, a_near, b, b_row, out):
    rows = a.shape[0]
    out[:rows] = (a[...].astype(f32) + a_near[...].astype(f32)).astype(bf16)
    out[rows:] = (b[...].astype(f32) + b_row[...].astype(f32)).astype(bf16)


def merge_kernel(flags, a, a_near, b, b_row, keep, give):
    upper = flags[3] == 1
    low = (a[...].astype(f32) + a_near[...].astype(f32)).astype(bf16)
    high = (b[...].astype(f32) + b_row[...].astype(f32)).astype(bf16)
    keep[...] = jnp.where(upper, high, low)
    give[...] = jnp.where(upper, low, high)


def transposed_kernel(left_ref, right_ref, out_ref):
    out_ref[...] = mm(left_ref[...], right_ref[...], TN).astype(bf16)


def transposed(left, right):
    count, width = left.shape
    model = right.shape[1]
    tile = 384 if width % 384 == 0 else min(256, width)
    return pl.pallas_call(
        transposed_kernel,
        grid=(width // tile,),
        in_specs=[
            pl.BlockSpec((count, tile), lambda i: (0, i)), pl.BlockSpec((count, model), lambda i: (0, 0))
        ],
        out_specs=pl.BlockSpec((tile, model), lambda i: (i, 0)),
        out_shape=jax.ShapeDtypeStruct((width, model), bf16),
        compiler_params=pltpu.CompilerParams(vmem_limit_bytes=40 * 2**20),
        cost_estimate=QUICK,
        name="transposed",
    )(left, right)


def placed(kernel, flags, operands, shapes, name):
    return pl.pallas_call(
        kernel,
        grid_spec=pltpu.PrefetchScalarGridSpec(
            num_scalar_prefetch=1,
            grid=(1,),
            in_specs=[pl.BlockSpec(o.shape, lambda i, f, n=o.ndim: (0,) * n) for o in operands],
            out_specs=[pl.BlockSpec(s.shape, lambda i, f, n=len(s.shape): (0,) * n) for s in shapes],
        ),
        out_shape=shapes,
        compiler_params=pltpu.CompilerParams(vmem_limit_bytes=40 * 2**20),
        cost_estimate=QUICK,
        name=name,
    )(flags, *operands)


def block(index, size):
    return pl.ds(pl.multiple_of(index * size, size), size)


def join_wide_kernel(flags, mine_ref, near_ref, core_mine_ref, core_near_ref, order_ref, out_ref):
    chip, core, place = flags[0], flags[1], flags[2]
    width, half = near_ref.shape[1], near_ref.shape[0] // 2
    own, away = block(core, half), block(1 - core, half)
    mine_at, near_at = 2 * place, 2 * (1 - place)
    for at, ref in ((mine_at + 1 - core, core_mine_ref), (near_at + core, near_ref), (near_at + 1 - core, core_near_ref)):
        out_ref[:half, block(at, width)] = ref[own, :]
        out_ref[half:, block(at, width)] = ref[away, :]
    out_ref[:half, block(mine_at + core, width)] = mine_ref[chip, own, :]
    out_ref[half:, block(mine_at + core, width)] = mine_ref[chip, away, :]


def give_core_kernel(flags, mine_ref, near_ref, out_ref):
    chip, core = flags[0], flags[1]
    width, half = near_ref.shape[1], near_ref.shape[0] // 2
    away = block(1 - core, half)
    out_ref[:, :width] = mine_ref[chip, away, :]
    out_ref[:, width:] = near_ref[away, :]


def join_own_kernel(flags, mine_ref, near_ref, core_ref, out_ref):
    chip, core, place = flags[0], flags[1], flags[2]
    width, half = near_ref.shape[1], near_ref.shape[0] // 2
    own = block(core, half)
    mine_at, near_at = 2 * place, 2 * (1 - place)
    out_ref[:, block(mine_at + core, width)] = mine_ref[chip, own, :]
    out_ref[:, block(near_at + core, width)] = near_ref[own, :]
    out_ref[:, block(mine_at + 1 - core, width)] = core_ref[:, :width]
    out_ref[:, block(near_at + 1 - core, width)] = core_ref[:, width:]


def split_core_kernel(flags, in_ref, keep_ref, send_ref):
    core = flags[1]
    width = in_ref.shape[1] // 4
    for part in range(2):
        cols = slice(part * width, (part + 1) * width)
        keep_ref[:, cols] = in_ref[:, block(2 * part + core, width)].astype(keep_ref.dtype)
        send_ref[:, cols] = in_ref[:, block(2 * part + 1 - core, width)].astype(send_ref.dtype)


def split_chip_kernel(flags, own_ref, away_ref, keep_ref, send_ref):
    core, place = flags[1], flags[2]
    half, width = own_ref.shape[0], own_ref.shape[1] // 2
    for rows, ref in ((block(core, half), own_ref), (block(1 - core, half), away_ref)):
        keep_ref[rows, :] = ref[:, block(place, width)]
        send_ref[rows, :] = ref[:, block(1 - place, width)]


def add_split_chip_kernel(flags, here_ref, there_ref, keep_ref, send_ref):
    core, place = flags[1], flags[2]
    half, width = here_ref.shape[0] // 2, here_ref.shape[1] // 2
    for rows, here, there in (
        (block(core, half), slice(0, half), slice(half, None)),
        (block(1 - core, half), slice(half, None), slice(0, half)),
    ):
        for ref, at in ((keep_ref, place), (send_ref, 1 - place)):
            cols = block(at, width)
            ref[rows, :] = (here_ref[here, cols] + there_ref[there, cols].astype(f32)).astype(bf16)


def join_sequences_kernel(flags, keep_ref, near_ref, out_ref):
    chip = flags[0]
    out_ref[chip] = keep_ref[...]
    out_ref[1 - chip] = near_ref[...]


def pick(values, index, axis=0):
    return lax.dynamic_index_in_dim(values, index, axis, keepdims=False)


def after(values, *others):
    return lax.optimization_barrier((values, *others))[0]


def hold(values, *arrived):
    return lax.optimization_barrier((values, *arrived))


def added(own, arrived):
    return (own.astype(f32) + arrived.astype(f32)).astype(bf16)


class PairSum:
    def __init__(self, values, give=None):
        self.values, self.give = values, give
        self.size = lax.axis_size("dp")
        self.index = lax.axis_index("dp")
        self.undo = []
        self.todo = []
        rows, bit = values.shape[0] * (1 if give is None else 2), 1
        while self.size & (self.size - 1) == 0 and bit < self.size and rows % 32 == 0:
            self.todo.append(("halve", bit))
            rows, bit = rows // 2, bit * 2
        if bit < self.size:
            self.todo.append(("rest", bit))
        self.todo += [("double", b) for kind, b in reversed(self.todo) if kind == "halve"]

    def send(self):
        kind, bit = self.todo[0]
        pairs = [(i, i ^ bit) for i in range(self.size)]
        upper = (self.index & bit) != 0
        if kind == "halve":
            if self.give is None:
                rows = self.values.shape[0] // 2
                low, high = self.values[:rows], self.values[rows:]
                self.values, self.give = jnp.where(upper, high, low), jnp.where(upper, low, high)
            self.arrived, self.give = lax.ppermute(self.give, "dp", pairs), None
        elif kind == "double":
            self.arrived = lax.ppermute(self.values, "dp", pairs)
        else:
            groups = [[i + bit * j for j in range(self.size // bit)] for i in range(bit)]
            self.arrived = lax.psum(self.values, "dp", axis_index_groups=groups)

    def receive(self):
        kind, bit = self.todo.pop(0)
        upper = (self.index & bit) != 0
        if kind == "halve":
            self.values = added(self.values, self.arrived)
        elif kind == "double":
            pair = (self.arrived, self.values), (self.values, self.arrived)
            self.values = jnp.where(upper, jnp.concatenate(pair[0]), jnp.concatenate(pair[1]))
        else:
            self.values = self.arrived

    def step(self, *others):
        if not self.todo:
            return others
        self.arrived, *others = hold(self.arrived, *others)
        self.receive()
        if self.todo:
            self.send()
        return others

    def finish(self):
        while self.todo:
            self.step()
        return self.values


def body(
    tokens, segments, w_qkv, qv_bias, w_out, out_bias, gain_one, shift_one,
    w_in, in_bias, w_down, down_bias, gain_two, shift_two, cotangent,
):
    row = lax.axis_index("row")
    col = lax.axis_index("col")
    chip, core = col // 2, col % 2
    same = row == chip
    first_core = core == 0
    flags = jnp.stack(
        [chip, core, jnp.where(same, 0, 1), lax.axis_index("dp") % 2]
    ).astype(jnp.int32)
    seq_count, count, width = tokens.shape
    half = count // 2
    model = width * lax.axis_size("col")
    heads = qv_bias.shape[0] // (2 * HEAD_DIM)
    hidden = in_bias.shape[0]
    cut, mid = 3 * heads * HEAD_DIM // 2, hidden // 2

    def shape(*dims, dtype=bf16):
        return jax.ShapeDtypeStruct(dims, dtype)

    qv_pairs = qv_bias.reshape(heads, 2, HEAD_DIM)
    qkv_bias = jnp.stack(
        [qv_pairs[:, 0], jnp.zeros_like(qv_pairs[:, 0]), qv_pairs[:, 1]], axis=1
    ).reshape(-1)
    vectors = jnp.concatenate([out_bias, gain_one, shift_one, down_bias, gain_two, shift_two])
    small = jnp.concatenate([vectors, qkv_bias, in_bias])
    small_near = to_chip(small)

    near = to_chip(pick(tokens, 1 - chip))
    qkv_row = to_row(w_qkv)
    core_mine = to_core(pick(tokens, chip))
    core_near = to_core(near)
    segment = pick(segments, chip).reshape(2, half)
    segment = jnp.concatenate([pick(segment, core), pick(segment, 1 - core)])
    ids = jnp.arange(HEAD_DIM)
    differs = jnp.where((segment[:, None] != ids) & (ids < 3), -(2.0**30), 0.0)
    mask = jnp.concatenate([differs, segment[:, None] == ids], axis=1).astype(bf16)

    qkv_own = after(w_qkv, near)
    near_a, near_b = to_chip(qkv_own[:, :cut]), to_chip(qkv_own[:, cut:])
    out_row = to_row(after(w_out, near))
    far_a = to_row(near_a)
    out_near = to_chip(after(w_out, near_a))
    wide = placed(
        join_wide_kernel, flags, [tokens, near, core_mine, core_near, near_a[:16, :128]],
        [shape(count, model)], "join_wide",
    )[0]
    wide, small_near, qkv_row, out_row = hold(wide, small_near, qkv_row, out_row)
    far_b = to_chip(qkv_row[:, cut:])
    out_far = to_chip(out_row)
    in_row = to_row(after(w_in, wide))
    wide_m, near_b = hold(wide, near_b)
    mine = attend(wide_m, w_qkv, qkv_row, qkv_bias, mask)
    qkv_bias_near = small_near[6 * width : 6 * width + 2 * cut]
    wide_a, far_a, far_b, out_near, out_far = hold(after(wide, mine[0]), far_a, far_b, out_near, out_far)
    in_near = to_chip(after(w_in, wide_a))
    down_row = to_row(after(w_down, wide_a))
    other_a = attend(wide_a, near_a, far_a, qkv_bias_near[:cut], mask)
    wide_b, in_row = hold(after(wide, other_a[0]), in_row)
    other_b = attend(wide_b, near_b, far_b, qkv_bias_near[cut:], mask)
    parts = [mine, other_a, other_b]
    lefts = [w_qkv, near_a, near_b]
    rights = [qkv_row, far_a, far_b]
    mixed = [mine[2], jnp.concatenate([other_a[2], other_b[2]], axis=1)]
    w_outs = [
        jnp.concatenate([w_out, out_row], axis=1), jnp.concatenate([out_near, out_far], axis=1)
    ]

    vec = vectors.reshape(6, width)
    vec_near = small_near[: 6 * width].reshape(6, width)
    low, high = jnp.where(same, vec, vec_near), jnp.where(same, vec_near, vec)
    both = jnp.concatenate([low, high], axis=1)
    there = to_core(after(both, mine[0]))
    even, odd = jnp.where(first_core, both, there), jnp.where(first_core, there, both)
    wide_vec = jnp.concatenate(
        [even[:, :width], odd[:, :width], even[:, width:], odd[:, width:]], axis=1
    )
    wide_vec = jnp.concatenate([wide_vec, jnp.zeros((2, model), f32)], axis=0)
    in_biases = [in_bias, small_near[6 * width + 2 * cut :]]

    def core_gather(values):
        return jnp.concatenate([values, to_core(values)], axis=0)

    mixed[0], mixed[1], down_row, in_near = hold(*mixed, down_row, in_near)
    in_far = to_row(in_near)
    down_near = to_chip(after(w_down, in_near))
    arrived = to_core(sum(mm(m[half:], w) for m, w in zip(mixed, w_outs)).astype(bf16))
    own = sum(mm(m[:half], w) for m, w in zip(mixed, w_outs))
    normed_one, inverse_one, first_out, first_low = by_rows(
        norm_one_kernel, flags, wide_vec, [wide[:half], own, arrived],
        [(model, f32), (128, f32), (model, f32), (model, bf16)], "norm_one",
    )
    first_wide = core_gather(first_low)

    act_mine, slope_mine = feed(first_wide, w_in, in_row, in_biases[0])
    down_mine = jnp.concatenate([w_down, down_row], axis=1)
    ffn_mine = [mm(act_mine[half:], down_mine), mm(act_mine[:half], down_mine)]
    ffn_mine[0], ffn_mine[1], in_far, down_near = hold(*ffn_mine, in_far, down_near)
    down_far_a = to_chip(after(down_row[:mid], down_near))
    down_far_b = to_row(down_near[mid:])
    cot_near = to_chip(after(pick(cotangent, 1 - chip), down_near))
    act_other, slope_other = feed(first_wide, in_near, in_far, in_biases[1])
    down_far = jnp.concatenate([down_far_a, down_far_b], axis=0)
    down_other = jnp.concatenate([down_near, down_far], axis=1)
    arrived = to_core((ffn_mine[0] + mm(act_other[half:], down_other)).astype(bf16))
    own = ffn_mine[1] + mm(act_other[:half], down_other)
    cot_give = placed(give_core_kernel, flags, [cotangent, cot_near], [shape(half, 2 * width)], "give_core")[0]
    cot_core = to_core(cot_give)
    cot = placed(
        join_own_kernel, flags, [cotangent, cot_near, cot_core], [shape(half, model)], "join_own"
    )[0]
    out_keep, out_give, grad_pre_two, grad_ffn, sums_two = by_rows(
        norm_two_kernel, flags, wide_vec, [first_out, own, arrived, cot],
        [(2 * width, bf16), (2 * width, bf16), (model, f32), (model, bf16), (0, f32)], "norm_two",
    )

    side = model // 2

    def second_sends(own_a, arrived_a, mine_b, arrived_b):
        rows = mine_b.shape[0]
        a_other, a_mine, b_own, b_away = pl.pallas_call(
            second_kernel,
            out_shape=[shape(rows, side)] * 4,
            compiler_params=pltpu.CompilerParams(vmem_limit_bytes=40 * 2**20),
            cost_estimate=QUICK,
            name="second",
        )(own_a, arrived_a, mine_b, arrived_b)
        return (a_mine, to_chip(a_other)), (b_own, to_row(b_away))

    def merged(a, a_near, b, b_row):
        return PairSum(*placed(merge_kernel, flags, [a, a_near, b, b_row], [shape(*a.shape)] * 2, "merge"))

    def joined(a, a_near, b, b_row):
        rows, cols = a.shape
        return pl.pallas_call(
            joined_kernel,
            out_shape=shape(2 * rows, cols),
            compiler_params=pltpu.CompilerParams(vmem_limit_bytes=40 * 2**20),
            cost_estimate=QUICK,
            name="joined",
        )(a, a_near, b, b_row)

    gw = core_gather(grad_ffn)
    down_away_a, down_own_a, down_other_b, down_mine_b = weight_grads(act_other, act_mine, gw)
    down_first = [to_row(down_away_a), to_chip(down_other_b)]
    hid_mine, in_sum_mine = feed_back(gw, w_down, down_row, slope_mine)
    hid_other, in_sum_other = feed_back(gw, down_near, down_far, slope_other)
    grad_in_biases = [in_sum_mine[0], in_sum_other[0]]
    in_mine = jnp.concatenate([w_in, in_row], axis=0)
    in_other = jnp.concatenate([in_near, in_far], axis=0)
    arrived = to_core((mm(hid_mine[half:], in_mine, NT) + mm(hid_other[half:], in_other, NT)).astype(bf16))
    own = mm(hid_mine[:half], in_mine, NT) + mm(hid_other[:half], in_other, NT)
    in_away_a, in_own_a, in_other_b, in_mine_b = weight_grads(hid_other, hid_mine, first_wide)
    own, arrived, *down_first = hold(own, arrived, *down_first)
    (da, da_near), (db, db_row) = second_sends(down_own_a, down_first[0], down_mine_b, down_first[1])
    own, da, db = hold(own, da, db)

    grad_pre_one, grad_attention, sums_one = by_rows(
        norm_back_kernel, flags, wide_vec, [grad_pre_two, own, arrived, normed_one, inverse_one],
        [(model, f32), (model, bf16), (0, f32)], "norm_back",
    )
    grad_attn_wide = core_gather(grad_attention)
    grad_mixed = [mm(grad_attn_wide, w, NT).astype(bf16) for w in w_outs[::-1]][::-1]
    narrow = grad_mixed[1].shape[1] // 2
    grad_outs = [transposed(m, grad_attn_wide) for m in mixed]
    grad_mixed[1], da_near, db_row = hold(grad_mixed[1], da_near, db_row)
    grad_down = joined(da, da_near, db, db_row)
    in_first = [to_row(after(in_away_a, grad_down)), to_chip(after(in_other_b, grad_down))]
    grad_down = lax.psum(grad_down, "dp")
    go_a = attend_back(*other_a, grad_mixed[1])
    wt_oa = transposed(go_a, wide)
    go_b = attend_back(*other_b, after(grad_mixed[1], wt_oa), at=1)
    gm, go_b, wt_oa, *in_first = hold(grad_mixed[0], go_b, wt_oa, *in_first)
    (ia, ia_near), (ib, ib_row) = second_sends(in_own_a, in_first[0], in_mine_b, in_first[1])
    wt_ob = transposed(after(go_b, ia), wide)
    qkv_a_other = to_row(after(wt_oa[:, side:], ia))
    gm_a = attend_back(*mine, after(gm, ia, ib, wt_ob))
    out_row_grads = to_row(jnp.concatenate([g[:, side:] for g in grad_outs[::-1]], axis=0))
    gm_a, ia_near, ib_row, grad_down = hold(gm_a, ia_near, ib_row, grad_down)
    sum_in = merged(ia, ia_near, ib, ib_row)
    sum_in.send()
    wt_ma = transposed(gm_a, wide)
    qkv_a_mine = to_row(wt_ma[:, side:])
    gm_b = attend_back(*mine, after(gm, wt_ma), first=1, at=1)
    gm_b, qkv_a_other, out_row_grads, qkv_a_mine = sum_in.step(gm_b, qkv_a_other, out_row_grads, qkv_a_mine)
    wt_mb = transposed(gm_b, wide)
    rows = grad_outs[0].shape[0]
    out_sums = added(
        jnp.concatenate([g[:, :side] for g in grad_outs[::-1]], axis=0), out_row_grads
    )
    out_near_grad = to_chip(out_sums[:rows])

    features = jnp.concatenate([sums_one[2:3], sums_one[:2], sums_two[2:3], sums_two[:2]], axis=0)
    f0, f1, f2, f3 = [features[:, i * width : (i + 1) * width] for i in range(4)]
    keep = jnp.concatenate([jnp.where(first_core, f0, f1), jnp.where(first_core, f2, f3)], axis=1)
    give = jnp.concatenate([jnp.where(first_core, f1, f0), jnp.where(first_core, f3, f2)], axis=1)
    features = keep + to_core(give)
    feature_mine = jnp.where(same, features[:, :width], features[:, width:])
    feature_near = jnp.where(same, features[:, width:], features[:, :width])
    extras = []
    for g, i, f in zip(((gm_a, gm_b), (go_a, go_b)), grad_in_biases, (feature_mine, feature_near)):
        sums = jnp.concatenate([jnp.sum(v, axis=0, dtype=f32) for v in g]).reshape(heads, 3, HEAD_DIM)
        sums = jnp.stack([sums[:, 0], sums[:, 2]], axis=1).reshape(-1)
        flat = jnp.concatenate([sums, i, f.reshape(-1)])
        lines = -(-flat.shape[0] // (64 * side)) * 64
        flat = jnp.pad(flat, (0, lines * side - flat.shape[0])).reshape(lines, side).astype(bf16)
        extras.append(jnp.concatenate([flat, flat], axis=1))

    b_near = to_chip(jnp.concatenate([wt_ob, extras[1]], axis=0))
    sum_mine = added(wt_ma[:, :side], qkv_a_mine)
    a_near = to_chip(added(wt_oa[:, :side], qkv_a_other))
    sum_b = added(jnp.concatenate([wt_mb, extras[0]], axis=0), b_near)
    b_row = to_row(sum_b[:, side:])
    grads = [jnp.concatenate([gm_a, after(gm_b, sum_b)], axis=1), go_a, go_b]
    grad_left, grad_right = [sum(mm(g, w, NT) for g, w in zip(grads, ws)) for ws in (lefts, rights)]
    grad_left, grad_right, b_row, a_near, out_near_grad = sum_in.step(grad_left, grad_right, b_row, a_near, out_near_grad)
    sum_qkv = PairSum(
        jnp.concatenate(
            [added(sum_mine, a_near), added(sum_b[:, :side], b_row), added(out_sums[rows:], out_near_grad)], axis=0
        )
    )
    sum_qkv.send()
    for _ in range(3):
        sum_in.step()
        sum_qkv.step()
    grad_in = sum_in.finish()
    summed = sum_qkv.finish().astype(f32)
    grad_w_down, grad_w_in = grad_down, grad_in
    grad_w_qkv = summed[: 2 * cut].T
    part_b = summed[2 * cut : -rows]
    grad_w_out = summed[-rows:]
    small = part_b.reshape(-1)
    qv_len = qv_bias.shape[0]
    g_qv, g_in = small[:qv_len], small[qv_len : qv_len + hidden]
    g_out, g_gone, g_sone, g_down, g_gtwo, g_stwo = small[
        qv_len + hidden : qv_len + hidden + 6 * width
    ].reshape(6, width)

    grad_wide = jnp.concatenate([grad_left, grad_right], axis=1)
    grad_wide = jnp.concatenate([grad_wide[:half] + grad_pre_one, grad_wide[half:]], axis=0)

    keep, give = placed(
        split_chip_kernel, flags, [out_keep, to_core(out_give)], [shape(count, width)] * 2, "split_chip"
    )
    output = placed(
        join_sequences_kernel, flags, [keep, to_chip(give)], [shape(2, count, width)], "join_sequences"
    )[0]
    keep, give = placed(
        split_core_kernel, flags, [grad_wide],
        [shape(count, 2 * width, dtype=f32), shape(count, 2 * width)], "split_core",
    )
    keep, give = placed(
        add_split_chip_kernel, flags, [keep, to_core(give)], [shape(count, width)] * 2, "add_split_chip"
    )
    grad_tokens = placed(
        join_sequences_kernel, flags, [keep, to_chip(give)], [shape(2, count, width)], "join_sequences"
    )[0]
    return (
        output, grad_tokens, grad_w_qkv, g_qv, grad_w_out, g_out, g_gone, g_sone,
        grad_w_in.astype(f32).T, g_in, grad_w_down.astype(f32), g_down, g_gtwo, g_stwo,
    )


def solution(mesh):
    tokens = P(("dp", "row"), None, "col")
    feature = P("col")
    by_row, by_col = P("row", "col"), P("col", "row")
    return jax.shard_map(
        body,
        mesh=mesh,
        in_specs=(
            tokens, P(("dp", "row"), None), by_row, feature, by_col, feature, feature, feature,
            by_row, feature, by_col, feature, feature, feature, tokens,
        ),
        out_specs=(
            tokens, tokens, by_row, feature, by_col, feature, feature, feature,
            by_row, feature, by_col, feature, feature, feature,
        ),
        check_vma=False,
    )
```

```python
import functools
import math

import jax
import jax.numpy as jnp
from jax import lax
from jax.experimental import pallas as pl
from jax.experimental.pallas import tpu as pltpu
from jax.sharding import PartitionSpec as P

HEAD_DIM = 64
epsilon = 1e-12
f32 = jnp.float32
bf16 = jnp.bfloat16
NT = (((1,), (1,)), ((), ()))
NN = (((1,), (0,)), ((), ()))
TN = (((0,), (0,)), ((), ()))


QUICK = pl.CostEstimate(flops=1024, bytes_accessed=1024, transcendentals=0)


def mm(left, right, dims=NN):
    return lax.dot_general(left, right, dims, preferred_element_type=f32)


def to_core(values):
    size = lax.axis_size("col")
    return lax.ppermute(values, "col", [(i, i ^ 1) for i in range(size)])


def to_chip(values):
    size = lax.axis_size("col")
    return lax.ppermute(values, "col", [(i, i ^ 2) for i in range(size)])


def to_row(values):
    return lax.ppermute(values, "row", [(0, 1), (1, 0)])


def attend_kernel(chunk, wide_ref, left_ref, right_ref, bias_ref, mask_ref, qkv_ref, exp_ref, mixed_ref, inv_ref):
    count, side = wide_ref.shape[0], left_ref.shape[0]
    projected = mm(wide_ref[:, :side], left_ref[...]) + mm(wide_ref[:, side:], right_ref[...])
    qkv_ref[...] = (projected + bias_ref[...]).astype(bf16)
    ones = jnp.ones((count, HEAD_DIM), bf16)
    for head in range(2):
        base = 3 * HEAD_DIM * head
        cols = slice(head * HEAD_DIM, (head + 1) * HEAD_DIM)
        query = qkv_ref[:, base : base + HEAD_DIM] * bf16(1.0 / math.sqrt(HEAD_DIM))
        key = qkv_ref[:, base + HEAD_DIM : base + 2 * HEAD_DIM]
        value = qkv_ref[:, base + 2 * HEAD_DIM : base + 3 * HEAD_DIM]
        query = jnp.concatenate([query, mask_ref[:, :HEAD_DIM]], axis=1)
        key = jnp.concatenate([key, mask_ref[:, HEAD_DIM:]], axis=1)
        value = jnp.concatenate([value, ones], axis=1)
        for start in range(0, count, chunk):
            rows = slice(start, start + chunk)
            scores = mm(query[rows], key, NT)
            top = jnp.max(scores, axis=-1, keepdims=True)
            exponent = jnp.exp(scores - top).astype(bf16)
            exp_ref[head, rows, :] = exponent
            mixed = mm(exponent, value)
            inverse = 1.0 / mixed[:, HEAD_DIM:]
            mixed_ref[rows, cols] = (mixed[:, :HEAD_DIM] * inverse).astype(bf16)
            inv_ref[rows, cols] = inverse


def attend(wide, left, right, bias, mask):
    count, model = wide.shape
    side, width = left.shape
    six = 6 * HEAD_DIM
    pairs = width // six
    return pl.pallas_call(
        functools.partial(attend_kernel, min(512, count)),
        grid=(pairs,),
        in_specs=[
            pl.BlockSpec((count, model), lambda p: (0, 0)),
            pl.BlockSpec((side, six), lambda p: (0, p)),
            pl.BlockSpec((side, six), lambda p: (0, p)),
            pl.BlockSpec((1, six), lambda p: (0, p)),
            pl.BlockSpec((count, 2 * HEAD_DIM), lambda p: (0, 0)),
        ],
        out_specs=[
            pl.BlockSpec((count, six), lambda p: (0, p)),
            pl.BlockSpec((2, count, count), lambda p: (p, 0, 0)),
            pl.BlockSpec((count, 2 * HEAD_DIM), lambda p: (0, p)),
            pl.BlockSpec((count, 2 * HEAD_DIM), lambda p: (0, p)),
        ],
        out_shape=[
            jax.ShapeDtypeStruct((count, width), bf16),
            jax.ShapeDtypeStruct((2 * pairs, count, count), bf16),
            jax.ShapeDtypeStruct((count, 2 * HEAD_DIM * pairs), bf16),
            jax.ShapeDtypeStruct((count, 2 * HEAD_DIM * pairs), f32),
        ],
        compiler_params=pltpu.CompilerParams(vmem_limit_bytes=52 * 2**20),
        cost_estimate=QUICK,
        name="attend",
    )(wide, left, right, bias.reshape(1, width), mask)


def attend_back_kernel(chunk, qkv_ref, exp_ref, mixed_ref, inv_ref, grad_ref, out_ref, sums_ref):
    count = qkv_ref.shape[0]
    lane = lax.broadcasted_iota(jnp.int32, (count, HEAD_DIM), 1)
    minus = jnp.where(lane < 2, -1.0, 0.0).astype(bf16)
    scale = 1.0 / math.sqrt(HEAD_DIM)
    for head in range(2):
        base = 3 * HEAD_DIM * head
        cols = slice(head * HEAD_DIM, (head + 1) * HEAD_DIM)
        query = qkv_ref[:, base : base + HEAD_DIM]
        key = qkv_ref[:, base + HEAD_DIM : base + 2 * HEAD_DIM]
        value = qkv_ref[:, base + 2 * HEAD_DIM : base + 3 * HEAD_DIM]
        value = jnp.concatenate([value, minus], axis=1)
        scaled = grad_ref[:, cols].astype(f32) * inv_ref[:, cols]
        scaled_low = scaled.astype(bf16)
        inner = jnp.sum(scaled * mixed_ref[:, cols].astype(f32), axis=1, keepdims=True)
        inner_high = inner.astype(bf16).astype(f32)
        inner_pair = jnp.where(
            lane == 0, inner_high, jnp.where(lane == 1, inner - inner_high, 0.0)
        ).astype(bf16)
        wide = jnp.concatenate([scaled_low, inner_pair], axis=1)
        grad_key = grad_value = None
        for start in range(0, count, chunk):
            rows = slice(start, start + chunk)
            exponent = exp_ref[head, rows, :]
            grad_probs = mm(wide[rows], value, NT)
            grad_scores = (exponent.astype(f32) * grad_probs).astype(bf16)
            out_ref[rows, base : base + HEAD_DIM] = (mm(grad_scores, key) * scale).astype(bf16)
            key_part = mm(query[rows], grad_scores, TN)
            value_part = mm(scaled_low[rows], exponent, TN)
            grad_key = key_part if grad_key is None else grad_key + key_part
            grad_value = value_part if grad_value is None else grad_value + value_part
        out_ref[:, base + HEAD_DIM : base + 2 * HEAD_DIM] = (grad_key.T * scale).astype(bf16)
        out_ref[:, base + 2 * HEAD_DIM : base + 3 * HEAD_DIM] = grad_value.T.astype(bf16)
    sums_ref[...] = mm(jnp.ones((8, count), bf16), out_ref[...])


def attend_back(qkv, exponent, mixed, inverse, grad_mixed, first=0, at=0):
    count, width = qkv.shape
    pairs, width = 1, 6 * HEAD_DIM
    return pl.pallas_call(
        functools.partial(attend_back_kernel, min(512, count)),
        grid=(pairs,),
        in_specs=[
            pl.BlockSpec((count, 6 * HEAD_DIM), lambda p: (0, p + first)),
            pl.BlockSpec((2, count, count), lambda p: (p + first, 0, 0)),
        ]
        + [pl.BlockSpec((count, 2 * HEAD_DIM), lambda p: (0, p + first))] * 2
        + [pl.BlockSpec((count, 2 * HEAD_DIM), lambda p: (0, p + at))],
        out_specs=[
            pl.BlockSpec((count, 6 * HEAD_DIM), lambda p: (0, p)),
            pl.BlockSpec((8, 6 * HEAD_DIM), lambda p: (0, p)),
        ],
        out_shape=[jax.ShapeDtypeStruct((count, width), bf16), jax.ShapeDtypeStruct((8, width), f32)],
        compiler_params=pltpu.CompilerParams(vmem_limit_bytes=48 * 2**20),
        cost_estimate=QUICK,
        name="attend_back",
    )(qkv, exponent, mixed, inverse, grad_mixed)


def centre(values):
    centered = values - jnp.mean(values, axis=-1, keepdims=True)
    inverse = lax.rsqrt(jnp.mean(centered * centered, axis=-1, keepdims=True) + epsilon)
    return centered * inverse, inverse


def centre_back(grad, normed, inverse):
    return inverse * (
        grad
        - jnp.mean(grad, axis=-1, keepdims=True)
        - normed * jnp.mean(grad * normed, axis=-1, keepdims=True)
    )


def keep_sums(sums_ref, *values):
    @pl.when(pl.program_id(0) == 0)
    def _():
        sums_ref[...] = jnp.zeros_like(sums_ref)

    for i, value in enumerate(values):
        sums_ref[i : i + 1, :] += jnp.sum(value, axis=0, keepdims=True)


def norm_one_kernel(flags, vec_ref, tokens_ref, own_ref, arrived_ref, normed_ref, inv_ref, first_ref, low_ref):
    values = tokens_ref[...].astype(f32) + own_ref[...] + arrived_ref[...].astype(f32) + vec_ref[0:1, :]
    normed, inverse = centre(values)
    first = normed * vec_ref[1:2, :] + vec_ref[2:3, :]
    normed_ref[...] = normed
    inv_ref[...] = jnp.broadcast_to(inverse, inv_ref.shape)
    first_ref[...] = first
    low_ref[...] = first.astype(bf16)


def norm_two_kernel(
    flags, vec_ref, first_ref, own_ref, arrived_ref, cot_ref, keep_ref, give_ref, grad_ref, low_ref, sums_ref
):
    core = flags[1]
    values = first_ref[...] + own_ref[...] + arrived_ref[...].astype(f32) + vec_ref[3:4, :]
    normed, inverse = centre(values)
    output = (normed * vec_ref[4:5, :] + vec_ref[5:6, :]).astype(bf16)
    width = output.shape[1] // 4
    for part in range(2):
        even = output[:, 2 * part * width : (2 * part + 1) * width]
        odd = output[:, (2 * part + 1) * width : (2 * part + 2) * width]
        cols = slice(part * width, (part + 1) * width)
        keep_ref[:, cols] = jnp.where(core == 0, even, odd)
        give_ref[:, cols] = jnp.where(core == 0, odd, even)
    cot = cot_ref[...].astype(f32)
    grad = centre_back(cot * vec_ref[4:5, :], normed, inverse)
    low = grad.astype(bf16)
    grad_ref[...] = grad
    low_ref[...] = low
    keep_sums(sums_ref, cot * normed, cot, low.astype(f32))


def norm_back_kernel(
    flags, vec_ref, above_ref, own_ref, arrived_ref, normed_ref, inv_ref, grad_ref, low_ref, sums_ref
):
    normed = normed_ref[...]
    above = above_ref[...] + own_ref[...] + arrived_ref[...].astype(f32)
    grad = centre_back(above * vec_ref[1:2, :], normed, inv_ref[:, :1])
    low = grad.astype(bf16)
    grad_ref[...] = grad
    low_ref[...] = low
    keep_sums(sums_ref, above * normed, above, low.astype(f32))


def by_rows(kernel, flags, vec, operands, outs, name):
    rows, model = operands[1].shape
    tile = min(128, rows)

    def spec(width):
        return pl.BlockSpec((tile, width), lambda i, f: (i, 0))

    shapes = [
        jax.ShapeDtypeStruct((rows, width) if width else (8, model), dtype) for width, dtype in outs
    ]
    return pl.pallas_call(
        kernel,
        grid_spec=pltpu.PrefetchScalarGridSpec(
            num_scalar_prefetch=1,
            grid=(rows // tile,),
            in_specs=[pl.BlockSpec(vec.shape, lambda i, f: (0, 0))] + [spec(o.shape[1]) for o in operands],
            out_specs=[
                spec(width) if width else pl.BlockSpec((8, model), lambda i, f: (0, 0))
                for width, _ in outs
            ],
        ),
        out_shape=shapes,
        compiler_params=pltpu.CompilerParams(vmem_limit_bytes=40 * 2**20),
        cost_estimate=QUICK,
        name=name,
    )(flags, vec, *operands)


def feed_kernel(wide_ref, left_ref, right_ref, bias_ref, act_ref, slope_ref):
    side = left_ref.shape[0]
    pre = mm(wide_ref[:, :side], left_ref[...]) + mm(wide_ref[:, side:], right_ref[...]) + bias_ref[...]
    cdf = 0.5 * (1.0 + lax.erf(pre * (1.0 / math.sqrt(2.0))))
    pdf = jnp.exp(-0.5 * pre * pre) * (1.0 / math.sqrt(2.0 * math.pi))
    act_ref[...] = (pre * cdf).astype(bf16)
    slope_ref[...] = (cdf + pre * pdf).astype(bf16)


def feed(wide, left, right, bias):
    count, model = wide.shape
    side, width = left.shape
    tile = min(256, width)
    cols = lambda rows: pl.BlockSpec((rows, tile), lambda i: (0, i))
    return pl.pallas_call(
        feed_kernel,
        grid=(width // tile,),
        in_specs=[pl.BlockSpec((count, model), lambda i: (0, 0)), cols(side), cols(side), cols(1)],
        out_specs=[cols(count), cols(count)],
        out_shape=[jax.ShapeDtypeStruct((count, width), bf16)] * 2,
        compiler_params=pltpu.CompilerParams(vmem_limit_bytes=40 * 2**20),
        cost_estimate=QUICK,
        name="feed",
    )(wide, left, right, bias.reshape(1, width))


def feed_back_kernel(grad_ref, left_ref, right_ref, slope_ref, out_ref, sums_ref):
    side = left_ref.shape[1]
    product = mm(grad_ref[:, :side], left_ref[...], NT) + mm(grad_ref[:, side:], right_ref[...], NT)
    low = (product * slope_ref[...].astype(f32)).astype(bf16)
    out_ref[...] = low
    sums_ref[...] = jnp.sum(low.astype(f32), axis=0, keepdims=True)


def feed_back(grad, left, right, slope):
    count, model = grad.shape
    width, side = left.shape
    tile = min(256, width)
    cols = lambda rows: pl.BlockSpec((rows, tile), lambda i: (0, i))
    rows = pl.BlockSpec((tile, side), lambda i: (i, 0))
    return pl.pallas_call(
        feed_back_kernel,
        grid=(width // tile,),
        in_specs=[pl.BlockSpec((count, model), lambda i: (0, 0)), rows, rows, cols(count)],
        out_specs=[cols(count), cols(1)],
        out_shape=[jax.ShapeDtypeStruct((count, width), bf16), jax.ShapeDtypeStruct((1, width), f32)],
        compiler_params=pltpu.CompilerParams(vmem_limit_bytes=40 * 2**20),
        cost_estimate=QUICK,
        name="feed_back",
    )(grad, left, right, slope)


def weight_kernel(other_ref, mine_ref, right_ref, away_ref, own_ref, other_out, mine_out):
    step, part = pl.program_id(0), pl.num_programs(0) // 4
    side = own_ref.shape[1]

    def product(ref):
        return mm(ref[...], right_ref[...], TN).astype(bf16)

    def split(ref):
        value = product(ref)
        own_ref[...] = value[:, :side]
        away_ref[...] = value[:, side:]

    @pl.when(step < part)
    def _():
        split(other_ref)

    @pl.when((step >= part) & (step < 2 * part))
    def _():
        other_out[...] = product(other_ref)

    @pl.when((step >= 2 * part) & (step < 3 * part))
    def _():
        split(mine_ref)

    @pl.when(step >= 3 * part)
    def _():
        mine_out[...] = product(mine_ref)


def weight_grads(other, mine, right):
    count, width = other.shape
    model = right.shape[1]
    side = model // 2
    tile = min(256, width // 2)
    n = width // tile
    p = n // 2

    def stacked(i):
        return jnp.where(i < p, i, jnp.where(i < 2 * p, p - 1, jnp.minimum(i - p, 2 * p - 1)))

    return pl.pallas_call(
        weight_kernel,
        grid=(2 * n,),
        in_specs=[
            pl.BlockSpec((count, tile), lambda i: (0, jnp.minimum(i, n - 1))),
            pl.BlockSpec((count, tile), lambda i: (0, jnp.maximum(i - n, 0))),
            pl.BlockSpec((count, model), lambda i: (0, 0)),
        ],
        out_specs=[
            pl.BlockSpec((tile, side), lambda i: (stacked(i), 0)),
            pl.BlockSpec((tile, side), lambda i: (stacked(i), 0)),
            pl.BlockSpec((tile, model), lambda i: (jnp.clip(i - p, 0, p - 1), 0)),
            pl.BlockSpec((tile, model), lambda i: (jnp.clip(i - 3 * p, 0, p - 1), 0)),
        ],
        out_shape=[jax.ShapeDtypeStruct((width, side), bf16)] * 2
        + [jax.ShapeDtypeStruct((width // 2, model), bf16)] * 2,
        compiler_params=pltpu.CompilerParams(vmem_limit_bytes=40 * 2**20),
        cost_estimate=QUICK,
        name="weight_grads",
    )(other, mine, right)


def second_kernel(own_a, arrived_a, mine_b, arrived_b, a_other, a_mine, b_own, b_away):
    size, side = a_mine.shape

    def added(x, y):
        return (x.astype(f32) + y.astype(f32)).astype(bf16)

    a_other[...] = added(own_a[:size], arrived_a[:size])
    a_mine[...] = added(own_a[size:], arrived_a[size:])
    b_own[...] = added(mine_b[:, :side], arrived_b[:, :side])
    b_away[...] = added(mine_b[:, side:], arrived_b[:, side:])


def joined_kernel(a, a_near, b, b_row, out):
    rows = a.shape[0]
    out[:rows] = (a[...].astype(f32) + a_near[...].astype(f32)).astype(bf16)
    out[rows:] = (b[...].astype(f32) + b_row[...].astype(f32)).astype(bf16)


def merge_kernel(flags, a, a_near, b, b_row, keep, give):
    upper = flags[3] == 1
    low = (a[...].astype(f32) + a_near[...].astype(f32)).astype(bf16)
    high = (b[...].astype(f32) + b_row[...].astype(f32)).astype(bf16)
    keep[...] = jnp.where(upper, high, low)
    give[...] = jnp.where(upper, low, high)


def transposed_kernel(left_ref, right_ref, out_ref):
    out_ref[...] = mm(left_ref[...], right_ref[...], TN).astype(bf16)


def transposed(left, right):
    count, width = left.shape
    model = right.shape[1]
    tile = 384 if width % 384 == 0 else min(256, width)
    return pl.pallas_call(
        transposed_kernel,
        grid=(width // tile,),
        in_specs=[
            pl.BlockSpec((count, tile), lambda i: (0, i)), pl.BlockSpec((count, model), lambda i: (0, 0))
        ],
        out_specs=pl.BlockSpec((tile, model), lambda i: (i, 0)),
        out_shape=jax.ShapeDtypeStruct((width, model), bf16),
        compiler_params=pltpu.CompilerParams(vmem_limit_bytes=40 * 2**20),
        cost_estimate=QUICK,
        name="transposed",
    )(left, right)


def placed(kernel, flags, operands, shapes, name):
    return pl.pallas_call(
        kernel,
        grid_spec=pltpu.PrefetchScalarGridSpec(
            num_scalar_prefetch=1,
            grid=(1,),
            in_specs=[pl.BlockSpec(o.shape, lambda i, f, n=o.ndim: (0,) * n) for o in operands],
            out_specs=[pl.BlockSpec(s.shape, lambda i, f, n=len(s.shape): (0,) * n) for s in shapes],
        ),
        out_shape=shapes,
        compiler_params=pltpu.CompilerParams(vmem_limit_bytes=40 * 2**20),
        cost_estimate=QUICK,
        name=name,
    )(flags, *operands)


def block(index, size):
    return pl.ds(pl.multiple_of(index * size, size), size)


def join_wide_kernel(flags, mine_ref, near_ref, core_mine_ref, core_near_ref, order_ref, out_ref):
    chip, core, place = flags[0], flags[1], flags[2]
    width, half = near_ref.shape[1], near_ref.shape[0] // 2
    own, away = block(core, half), block(1 - core, half)
    mine_at, near_at = 2 * place, 2 * (1 - place)
    for at, ref in ((mine_at + 1 - core, core_mine_ref), (near_at + core, near_ref), (near_at + 1 - core, core_near_ref)):
        out_ref[:half, block(at, width)] = ref[own, :]
        out_ref[half:, block(at, width)] = ref[away, :]
    out_ref[:half, block(mine_at + core, width)] = mine_ref[chip, own, :]
    out_ref[half:, block(mine_at + core, width)] = mine_ref[chip, away, :]


def give_core_kernel(flags, mine_ref, near_ref, out_ref):
    chip, core = flags[0], flags[1]
    width, half = near_ref.shape[1], near_ref.shape[0] // 2
    away = block(1 - core, half)
    out_ref[:, :width] = mine_ref[chip, away, :]
    out_ref[:, width:] = near_ref[away, :]


def join_own_kernel(flags, mine_ref, near_ref, core_ref, out_ref):
    chip, core, place = flags[0], flags[1], flags[2]
    width, half = near_ref.shape[1], near_ref.shape[0] // 2
    own = block(core, half)
    mine_at, near_at = 2 * place, 2 * (1 - place)
    out_ref[:, block(mine_at + core, width)] = mine_ref[chip, own, :]
    out_ref[:, block(near_at + core, width)] = near_ref[own, :]
    out_ref[:, block(mine_at + 1 - core, width)] = core_ref[:, :width]
    out_ref[:, block(near_at + 1 - core, width)] = core_ref[:, width:]


def split_core_kernel(flags, in_ref, keep_ref, send_ref):
    core = flags[1]
    width = in_ref.shape[1] // 4
    for part in range(2):
        cols = slice(part * width, (part + 1) * width)
        keep_ref[:, cols] = in_ref[:, block(2 * part + core, width)].astype(keep_ref.dtype)
        send_ref[:, cols] = in_ref[:, block(2 * part + 1 - core, width)].astype(send_ref.dtype)


def split_chip_kernel(flags, own_ref, away_ref, keep_ref, send_ref):
    core, place = flags[1], flags[2]
    half, width = own_ref.shape[0], own_ref.shape[1] // 2
    for rows, ref in ((block(core, half), own_ref), (block(1 - core, half), away_ref)):
        keep_ref[rows, :] = ref[:, block(place, width)]
        send_ref[rows, :] = ref[:, block(1 - place, width)]


def add_split_chip_kernel(flags, here_ref, there_ref, keep_ref, send_ref):
    core, place = flags[1], flags[2]
    half, width = here_ref.shape[0] // 2, here_ref.shape[1] // 2
    for rows, here, there in (
        (block(core, half), slice(0, half), slice(half, None)),
        (block(1 - core, half), slice(half, None), slice(0, half)),
    ):
        for ref, at in ((keep_ref, place), (send_ref, 1 - place)):
            cols = block(at, width)
            ref[rows, :] = (here_ref[here, cols] + there_ref[there, cols].astype(f32)).astype(bf16)


def join_sequences_kernel(flags, keep_ref, near_ref, out_ref):
    chip = flags[0]
    out_ref[chip] = keep_ref[...]
    out_ref[1 - chip] = near_ref[...]


def pick(values, index, axis=0):
    return lax.dynamic_index_in_dim(values, index, axis, keepdims=False)


def after(values, *others):
    return lax.optimization_barrier((values, *others))[0]


def hold(values, *arrived):
    return lax.optimization_barrier((values, *arrived))


def added(own, arrived):
    return (own.astype(f32) + arrived.astype(f32)).astype(bf16)


class PairSum:
    def __init__(self, values, give=None):
        self.values, self.give = values, give
        self.size = lax.axis_size("dp")
        self.index = lax.axis_index("dp")
        self.undo = []
        self.todo = []
        rows, bit = values.shape[0] * (1 if give is None else 2), 1
        while self.size & (self.size - 1) == 0 and bit < self.size and rows % 32 == 0:
            self.todo.append(("halve", bit))
            rows, bit = rows // 2, bit * 2
        if bit < self.size:
            self.todo.append(("rest", bit))
        self.todo += [("double", b) for kind, b in reversed(self.todo) if kind == "halve"]

    def send(self):
        kind, bit = self.todo[0]
        pairs = [(i, i ^ bit) for i in range(self.size)]
        upper = (self.index & bit) != 0
        if kind == "halve":
            if self.give is None:
                rows = self.values.shape[0] // 2
                low, high = self.values[:rows], self.values[rows:]
                self.values, self.give = jnp.where(upper, high, low), jnp.where(upper, low, high)
            self.arrived, self.give = lax.ppermute(self.give, "dp", pairs), None
        elif kind == "double":
            self.arrived = lax.ppermute(self.values, "dp", pairs)
        else:
            groups = [[i + bit * j for j in range(self.size // bit)] for i in range(bit)]
            self.arrived = lax.psum(self.values, "dp", axis_index_groups=groups)

    def receive(self):
        kind, bit = self.todo.pop(0)
        upper = (self.index & bit) != 0
        if kind == "halve":
            self.values = added(self.values, self.arrived)
        elif kind == "double":
            pair = (self.arrived, self.values), (self.values, self.arrived)
            self.values = jnp.where(upper, jnp.concatenate(pair[0]), jnp.concatenate(pair[1]))
        else:
            self.values = self.arrived

    def step(self, *others):
        if not self.todo:
            return others
        self.arrived, *others = hold(self.arrived, *others)
        self.receive()
        if self.todo:
            self.send()
        return others

    def finish(self):
        while self.todo:
            self.step()
        return self.values


def body(
    tokens, segments, w_qkv, qv_bias, w_out, out_bias, gain_one, shift_one,
    w_in, in_bias, w_down, down_bias, gain_two, shift_two, cotangent,
):
    row = lax.axis_index("row")
    col = lax.axis_index("col")
    chip, core = col // 2, col % 2
    same = row == chip
    first_core = core == 0
    flags = jnp.stack(
        [chip, core, jnp.where(same, 0, 1), lax.axis_index("dp") % 2]
    ).astype(jnp.int32)
    seq_count, count, width = tokens.shape
    half = count // 2
    model = width * lax.axis_size("col")
    heads = qv_bias.shape[0] // (2 * HEAD_DIM)
    hidden = in_bias.shape[0]
    cut, mid = 3 * heads * HEAD_DIM // 2, hidden // 2

    def shape(*dims, dtype=bf16):
        return jax.ShapeDtypeStruct(dims, dtype)

    qv_pairs = qv_bias.reshape(heads, 2, HEAD_DIM)
    qkv_bias = jnp.stack(
        [qv_pairs[:, 0], jnp.zeros_like(qv_pairs[:, 0]), qv_pairs[:, 1]], axis=1
    ).reshape(-1)
    vectors = jnp.concatenate([out_bias, gain_one, shift_one, down_bias, gain_two, shift_two])
    small = jnp.concatenate([vectors, qkv_bias, in_bias])
    small_near = to_chip(small)

    near = to_chip(pick(tokens, 1 - chip))
    qkv_row = to_row(w_qkv)
    core_mine = to_core(pick(tokens, chip))
    core_near = to_core(near)
    segment = pick(segments, chip).reshape(2, half)
    segment = jnp.concatenate([pick(segment, core), pick(segment, 1 - core)])
    ids = jnp.arange(HEAD_DIM)
    differs = jnp.where((segment[:, None] != ids) & (ids < 3), -(2.0**30), 0.0)
    mask = jnp.concatenate([differs, segment[:, None] == ids], axis=1).astype(bf16)

    qkv_own = after(w_qkv, near)
    near_a, near_b = to_chip(qkv_own[:, :cut]), to_chip(qkv_own[:, cut:])
    out_row = to_row(after(w_out, near))
    far_a = to_row(near_a)
    out_near = to_chip(after(w_out, near_a))
    wide = placed(
        join_wide_kernel, flags, [tokens, near, core_mine, core_near, near_a[:16, :128]],
        [shape(count, model)], "join_wide",
    )[0]
    wide, small_near, qkv_row, out_row = hold(wide, small_near, qkv_row, out_row)
    far_b = to_chip(qkv_row[:, cut:])
    out_far = to_chip(out_row)
    in_row = to_row(after(w_in, wide))
    wide_m, near_b = hold(wide, near_b)
    mine = attend(wide_m, w_qkv, qkv_row, qkv_bias, mask)
    qkv_bias_near = small_near[6 * width : 6 * width + 2 * cut]
    wide_a, far_a, far_b, out_near, out_far = hold(after(wide, mine[0]), far_a, far_b, out_near, out_far)
    in_near = to_chip(after(w_in, wide_a))
    down_row = to_row(after(w_down, wide_a))
    other_a = attend(wide_a, near_a, far_a, qkv_bias_near[:cut], mask)
    wide_b, in_row = hold(after(wide, other_a[0]), in_row)
    other_b = attend(wide_b, near_b, far_b, qkv_bias_near[cut:], mask)
    parts = [mine, other_a, other_b]
    lefts = [w_qkv, near_a, near_b]
    rights = [qkv_row, far_a, far_b]
    mixed = [mine[2], jnp.concatenate([other_a[2], other_b[2]], axis=1)]
    w_outs = [
        jnp.concatenate([w_out, out_row], axis=1), jnp.concatenate([out_near, out_far], axis=1)
    ]

    vec = vectors.reshape(6, width)
    vec_near = small_near[: 6 * width].reshape(6, width)
    low, high = jnp.where(same, vec, vec_near), jnp.where(same, vec_near, vec)
    both = jnp.concatenate([low, high], axis=1)
    there = to_core(after(both, mine[0]))
    even, odd = jnp.where(first_core, both, there), jnp.where(first_core, there, both)
    wide_vec = jnp.concatenate(
        [even[:, :width], odd[:, :width], even[:, width:], odd[:, width:]], axis=1
    )
    wide_vec = jnp.concatenate([wide_vec, jnp.zeros((2, model), f32)], axis=0)
    in_biases = [in_bias, small_near[6 * width + 2 * cut :]]

    def core_gather(values):
        return jnp.concatenate([values, to_core(values)], axis=0)

    mixed[0], mixed[1], down_row, in_near = hold(*mixed, down_row, in_near)
    in_far = to_row(in_near)
    down_near = to_chip(after(w_down, in_near))
    arrived = to_core(sum(mm(m[half:], w) for m, w in zip(mixed, w_outs)).astype(bf16))
    own = sum(mm(m[:half], w) for m, w in zip(mixed, w_outs))
    own, in_far, down_near = hold(own, in_far, down_near)
    cot_near = to_chip(after(pick(cotangent, 1 - chip), down_near))
    down_far_a = to_chip(after(down_row[: mid // 2], down_near))
    down_far_b = to_row(down_near[mid // 2 :])
    normed_one, inverse_one, first_out, first_low = by_rows(
        norm_one_kernel, flags, wide_vec, [wide[:half], own, arrived],
        [(model, f32), (128, f32), (model, f32), (model, bf16)], "norm_one",
    )
    first_wide = core_gather(first_low)

    act_mine, slope_mine = feed(first_wide, w_in, in_row, in_biases[0])
    down_mine = jnp.concatenate([w_down, down_row], axis=1)
    act_mine, cot_near = hold(act_mine, cot_near)
    ffn_mine = [mm(act_mine[half:], down_mine), mm(act_mine[:half], down_mine)]
    act_other, slope_other = feed(first_wide, in_near, in_far, in_biases[1])
    act_other, down_far_a, down_far_b = hold(act_other, down_far_a, down_far_b)
    down_far = jnp.concatenate([down_far_a, down_far_b], axis=0)
    down_other = jnp.concatenate([down_near, down_far], axis=1)
    arrived = to_core((ffn_mine[0] + mm(act_other[half:], down_other)).astype(bf16))
    own = ffn_mine[1] + mm(act_other[:half], down_other)
    cot_give = placed(give_core_kernel, flags, [cotangent, cot_near], [shape(half, 2 * width)], "give_core")[0]
    cot_core = to_core(cot_give)
    cot = placed(
        join_own_kernel, flags, [cotangent, cot_near, cot_core], [shape(half, model)], "join_own"
    )[0]
    out_keep, out_give, grad_pre_two, grad_ffn, sums_two = by_rows(
        norm_two_kernel, flags, wide_vec, [first_out, own, arrived, cot],
        [(2 * width, bf16), (2 * width, bf16), (model, f32), (model, bf16), (0, f32)], "norm_two",
    )

    out_away = to_core(out_give)
    side = model // 2

    def second_sends(own_a, arrived_a, mine_b, arrived_b):
        rows = mine_b.shape[0]
        a_other, a_mine, b_own, b_away = pl.pallas_call(
            second_kernel,
            out_shape=[shape(rows, side)] * 4,
            compiler_params=pltpu.CompilerParams(vmem_limit_bytes=40 * 2**20),
            cost_estimate=QUICK,
            name="second",
        )(own_a, arrived_a, mine_b, arrived_b)
        return (a_mine, to_chip(a_other)), (b_own, to_row(b_away))

    def merged(a, a_near, b, b_row):
        return PairSum(*placed(merge_kernel, flags, [a, a_near, b, b_row], [shape(*a.shape)] * 2, "merge"))

    def joined(a, a_near, b, b_row):
        rows, cols = a.shape
        return pl.pallas_call(
            joined_kernel,
            out_shape=shape(2 * rows, cols),
            compiler_params=pltpu.CompilerParams(vmem_limit_bytes=40 * 2**20),
            cost_estimate=QUICK,
            name="joined",
        )(a, a_near, b, b_row)

    gw = core_gather(grad_ffn)
    down_away_a, down_own_a, down_other_b, down_mine_b = weight_grads(act_other, act_mine, gw)
    down_first = [to_row(down_away_a), to_chip(down_other_b)]
    hid_mine, in_sum_mine = feed_back(gw, w_down, down_row, slope_mine)
    hid_other, in_sum_other = feed_back(gw, down_near, down_far, slope_other)
    grad_in_biases = [in_sum_mine[0], in_sum_other[0]]
    in_mine = jnp.concatenate([w_in, in_row], axis=0)
    in_other = jnp.concatenate([in_near, in_far], axis=0)
    arrived = to_core((mm(hid_mine[half:], in_mine, NT) + mm(hid_other[half:], in_other, NT)).astype(bf16))
    own = mm(hid_mine[:half], in_mine, NT) + mm(hid_other[:half], in_other, NT)
    in_away_a, in_own_a, in_other_b, in_mine_b = weight_grads(hid_other, hid_mine, first_wide)
    own, arrived, out_away, *down_first = hold(own, arrived, out_away, *down_first)
    out_keep, out_give = placed(
        split_chip_kernel, flags, [out_keep, out_away], [shape(count, width)] * 2, "split_chip"
    )
    (da, da_near), (db, db_row) = second_sends(down_own_a, down_first[0], down_mine_b, down_first[1])
    own, da, db = hold(own, da, db)

    grad_pre_one, grad_attention, sums_one = by_rows(
        norm_back_kernel, flags, wide_vec, [grad_pre_two, own, arrived, normed_one, inverse_one],
        [(model, f32), (model, bf16), (0, f32)], "norm_back",
    )
    grad_attn_wide = core_gather(grad_attention)
    grad_mixed = [mm(grad_attn_wide, w, NT).astype(bf16) for w in w_outs[::-1]][::-1]
    narrow = grad_mixed[1].shape[1] // 2
    grad_outs = [transposed(m, grad_attn_wide) for m in mixed]
    grad_mixed[1], da_near, db_row = hold(grad_mixed[1], da_near, db_row)
    grad_down = joined(da, da_near, db, db_row)
    in_first = [to_row(after(in_away_a, grad_down)), to_chip(after(in_other_b, grad_down))]
    grad_down = lax.psum(grad_down, "dp")
    go_a, sum_oa = attend_back(*other_a, grad_mixed[1])
    out_near_seq = to_chip(after(out_give, go_a))
    wt_oa = transposed(go_a, wide)
    go_b, sum_ob = attend_back(*other_b, after(grad_mixed[1], wt_oa), at=1)
    gm, go_b, wt_oa, out_near_seq, *in_first = hold(grad_mixed[0], go_b, wt_oa, out_near_seq, *in_first)
    output = placed(
        join_sequences_kernel, flags, [out_keep, out_near_seq], [shape(2, count, width)], "join_sequences"
    )[0]
    (ia, ia_near), (ib, ib_row) = second_sends(in_own_a, in_first[0], in_mine_b, in_first[1])
    wt_ob = transposed(after(go_b, ia), wide)
    qkv_a_other = to_row(after(wt_oa[:, side:], ia))
    gm_a, sum_ma = attend_back(*mine, after(gm, ia, ib, wt_ob))
    out_row_grads = to_row(jnp.concatenate([g[:, side:] for g in grad_outs[::-1]], axis=0))
    gm_a, ia_near, ib_row, qkv_a_other, out_row_grads = hold(gm_a, ia_near, ib_row, qkv_a_other, out_row_grads)
    a_near = to_chip(added(wt_oa[:, :side], qkv_a_other))
    rows = grad_outs[0].shape[0]
    out_sums = added(
        jnp.concatenate([g[:, :side] for g in grad_outs[::-1]], axis=0), out_row_grads
    )
    out_near_grad = to_chip(out_sums[:rows])
    sum_in = merged(ia, ia_near, ib, ib_row)
    sum_in.send()
    wt_ma = transposed(gm_a, wide)
    qkv_a_mine = to_row(wt_ma[:, side:])
    gm_b, sum_mb = attend_back(*mine, after(gm, wt_ma), first=1, at=1)
    gm_b, a_near, qkv_a_mine, grad_down = sum_in.step(gm_b, a_near, qkv_a_mine, grad_down)
    wt_mb = transposed(gm_b, wide)

    features = jnp.concatenate([sums_one[2:3], sums_one[:2], sums_two[2:3], sums_two[:2]], axis=0)
    f0, f1, f2, f3 = [features[:, i * width : (i + 1) * width] for i in range(4)]
    keep = jnp.concatenate([jnp.where(first_core, f0, f1), jnp.where(first_core, f2, f3)], axis=1)
    give = jnp.concatenate([jnp.where(first_core, f1, f0), jnp.where(first_core, f3, f2)], axis=1)
    features = keep + to_core(give)
    feature_mine = jnp.where(same, features[:, :width], features[:, width:])
    feature_near = jnp.where(same, features[:, width:], features[:, :width])
    extras = []
    for g, i, f in zip(((sum_ma, sum_mb), (sum_oa, sum_ob)), grad_in_biases, (feature_mine, feature_near)):
        sums = jnp.concatenate([v[0] for v in g])
        three = 3 * HEAD_DIM
        sums = jnp.concatenate(
            [sums[three * h + at : three * h + at + HEAD_DIM] for h in range(heads) for at in (0, 2 * HEAD_DIM)]
        )
        flat = jnp.concatenate([sums, i, f.reshape(-1)])
        lines = -(-flat.shape[0] // (64 * side)) * 64
        flat = jnp.pad(flat, (0, lines * side - flat.shape[0])).reshape(lines, side).astype(bf16)
        extras.append(jnp.concatenate([flat, flat], axis=1))

    b_near = to_chip(jnp.concatenate([wt_ob, extras[1]], axis=0))
    sum_mine = added(wt_ma[:, :side], qkv_a_mine)
    sum_b = added(jnp.concatenate([wt_mb, extras[0]], axis=0), b_near)
    b_row = to_row(sum_b[:, side:])
    grads = [jnp.concatenate([gm_a, after(gm_b, sum_b)], axis=1), go_a, go_b]
    grad_left, grad_right = [sum(mm(g, w, NT) for g, w in zip(grads, ws)) for ws in (lefts, rights)]
    grad_left, grad_right, b_row, out_near_grad = sum_in.step(grad_left, grad_right, b_row, out_near_grad)
    sum_qkv = PairSum(
        jnp.concatenate(
            [added(sum_mine, a_near), added(sum_b[:, :side], b_row), added(out_sums[rows:], out_near_grad)], axis=0
        )
    )
    sum_qkv.send()
    while sum_in.todo and sum_qkv.todo:
        sum_in.arrived, sum_qkv.arrived = hold(sum_in.arrived, sum_qkv.arrived)
        for one in (sum_qkv, sum_in):
            one.receive()
            if one.todo:
                one.send()
    grad_in = sum_in.finish()
    summed = sum_qkv.finish().astype(f32)
    grad_w_down, grad_w_in = grad_down, grad_in
    grad_w_qkv = summed[: 2 * cut].T
    part_b = summed[2 * cut : -rows]
    grad_w_out = summed[-rows:]
    small = part_b.reshape(-1)
    qv_len = qv_bias.shape[0]
    g_qv, g_in = small[:qv_len], small[qv_len : qv_len + hidden]
    g_out, g_gone, g_sone, g_down, g_gtwo, g_stwo = small[
        qv_len + hidden : qv_len + hidden + 6 * width
    ].reshape(6, width)

    grad_wide = jnp.concatenate([grad_left, grad_right], axis=1)
    grad_wide = jnp.concatenate([grad_wide[:half] + grad_pre_one, grad_wide[half:]], axis=0)

    keep, give = placed(
        split_core_kernel, flags, [grad_wide],
        [shape(count, 2 * width, dtype=f32), shape(count, 2 * width)], "split_core",
    )
    keep, give = placed(
        add_split_chip_kernel, flags, [keep, to_core(give)], [shape(count, width)] * 2, "add_split_chip"
    )
    grad_tokens = placed(
        join_sequences_kernel, flags, [keep, to_chip(give)], [shape(2, count, width)], "join_sequences"
    )[0]
    return (
        output, grad_tokens, grad_w_qkv, g_qv, grad_w_out, g_out, g_gone, g_sone,
        grad_w_in.astype(f32).T, g_in, grad_w_down.astype(f32), g_down, g_gtwo, g_stwo,
    )


def solution(mesh):
    tokens = P(("dp", "row"), None, "col")
    feature = P("col")
    by_row, by_col = P("row", "col"), P("col", "row")
    return jax.shard_map(
        body,
        mesh=mesh,
        in_specs=(
            tokens, P(("dp", "row"), None), by_row, feature, by_col, feature, feature, feature,
            by_row, feature, by_col, feature, feature, feature, tokens,
        ),
        out_specs=(
            tokens, tokens, by_row, feature, by_col, feature, feature, feature,
            by_row, feature, by_col, feature, feature, feature,
        ),
        check_vma=False,
    )
```
